512 devices in a mesh: depth: 8 (over z), lat: 64 (over y, x, core).
Axes of the slice: x: 4, y: 8, z: 8, core: 2. Of those that a mesh axis runs over, the one named last changes fastest.
Arguments:
- volume: bfloat16 [8, 4096, 4096], P('depth', 'lat'), may hold values from -6 to 6
- hologram: bfloat16 [4096, 4096], P('lat'), may hold values from -6 to 6
- plane_depth: float32 [8], P('depth'), may hold values from 1 to 4
- tile_list: int32 [8, 32, 16], P('depth'), may hold values from 0 to 32, as said below
Outputs:
- new_volume: float32 [8, 4096, 4096], P('depth', 'lat')
The draws below stay inside these ranges and needn't reach their ends.
Inputs may be any that keep to these rules, and one draw needn't show every extreme that they name: `tile_list`: each list names distinct column tiles; the value 32 marks an unused slot, and unused slots come after the used ones; every plane has a tile row whose list is full and one that names a single tile.
All inputs are finite; a program needn't handle non-finite values.
Results may differ from the reference program's by a relative error of at most 0.0003.
Values sent between devices are 32-bit elements; how exact they have to be, the bound alone decides.
No kernel may reach another device: no remote copies, remote signals or barrier semaphores. Data moves between devices by JAX's collectives and lax.ppermute only.
A program may use at most 64 MiB of HBM per device.

```python
import math
import jax
import jax.numpy as jnp
from jax import lax

NR = 4096
NC = 4096
TILE = 128
MAXT = 16
PLANES = 8
TROWS = 32
TCOLS = 32


def draw_tile_list(key, part):
    key = jax.random.fold_in(key, 17)
    subkeys = jax.random.split(key, 4)
    scores = jax.random.randint(subkeys[0], (PLANES, TROWS, TCOLS), 0, 1 << 20)
    scores = scores * TCOLS + lax.broadcasted_iota(jnp.int32, (PLANES, TROWS, TCOLS), 2)
    ordering = jnp.argsort(scores, axis=-1).astype(jnp.int32)[:, :, :MAXT]
    plane_level = jax.random.randint(subkeys[1], (PLANES, 1), 1, 5)
    row_spread = jax.random.randint(subkeys[2], (PLANES, TROWS), 1, MAXT + 1)
    used_count = jnp.clip(row_spread * plane_level // 4, 1, MAXT)
    full_row = jax.random.randint(subkeys[3], (PLANES, 1), 0, TROWS)
    row_ids = lax.broadcasted_iota(jnp.int32, (PLANES, TROWS), 1)
    used_count = jnp.where(row_ids == full_row, MAXT, used_count)
    used_count = jnp.where(row_ids == (full_row + 1) % TROWS, 1, used_count)
    slot_ids = lax.broadcasted_iota(jnp.int32, (PLANES, TROWS, MAXT), 2)
    return jnp.where(slot_ids < used_count[:, :, None], ordering, TCOLS).astype(jnp.int32)


def levels(key, shape, shards, low, top_value):
    gain = 1.0
    for position, shards_of in shards:
        steps = jax.random.uniform(jax.random.fold_in(jax.random.fold_in(key, 6), position), (shards_of,), jnp.float32, low / len(shards), top_value / len(shards))
        gain = gain * jnp.repeat(jnp.exp(steps), shape[position] // shards_of).reshape((-1,) + (1,) * (len(shape) - 1 - position))
    return gain


def scatter_about(rng, dims, spread, reach, cuts=(), held_as=jnp.bfloat16):
    array = spread * jax.random.normal(rng, dims, jnp.float32)
    if cuts:
        array = array * levels(rng, dims, cuts, -0.22, 0.18)
    return jnp.clip(array, -reach, reach).astype(held_as)


def setup_inputs(seed: int = 0) -> dict:
    key_of = jax.random.split(jax.random.key(seed), 5)
    volume = scatter_about(key_of[0], (PLANES, NR, NC), 1.0, 6.0, ((0, 8), (1, 64)))
    hologram = scatter_about(key_of[1], (NR, NC), 1.0, 6.0, ((0, 64),))
    plane_depth = jnp.clip(jnp.exp(math.log(4.0) - 1.3862944 * jax.random.uniform(key_of[2], (PLANES,), jnp.float32) ** levels(key_of[2], (PLANES,), ((0, 8),), -0.2, 0.2)), 1.0, 4.0)
    tile_list = draw_tile_list(jax.random.fold_in(key_of[4], 71), 0)
    return dict(volume=volume, hologram=hologram, plane_depth=plane_depth, tile_list=tile_list)


TWO_PI = 2.0 * math.pi
WAVE_RATIO = 0.266
DEPTH_SCALE = 0.001 / 5.32e-07
STEP_SIZE = 0.1
THRESHOLD = 0.25

def signed_freq(index_ids, length):
    return jnp.where(index_ids < length // 2, index_ids, index_ids - length)

def bending_table(row_freq, col_freq, total_rows, total_cols):
    freq_rows = signed_freq(row_freq, total_rows).astype(jnp.float32) * (WAVE_RATIO / total_rows)
    freq_cols = signed_freq(col_freq, total_cols).astype(jnp.float32) * (WAVE_RATIO / total_cols)
    squared = freq_rows[:, None] * freq_rows[:, None] + freq_cols[None, :] * freq_cols[None, :]
    return squared / (1.0 + jnp.sqrt(1.0 - squared))

def reference(volume, hologram, plane_depth, tile_list):
    bending = bending_table(jnp.arange(NR, dtype=jnp.int32), jnp.arange(NC, dtype=jnp.int32), NR, NC)
    tile_ids = jnp.arange(NC // TILE, dtype=jnp.int32)

    def support_of(plane_idx):
        tile_hits = jnp.any(tile_list[plane_idx][:, :, None] == tile_ids[None, None, :], axis=1)
        return jnp.repeat(jnp.repeat(tile_hits, TILE, axis=0), TILE, axis=1).astype(jnp.float32)

    def wave_of(plane_idx):
        phases = -(TWO_PI * DEPTH_SCALE * plane_depth[plane_idx]) * bending
        return (jnp.cos(phases), jnp.sin(phases))
    field_sum = jnp.zeros((NR, NC), jnp.float32)
    for plane_idx in range(PLANES):
        current = volume[plane_idx].astype(jnp.float32) * support_of(plane_idx)
        wave_cos, wave_sin = wave_of(plane_idx)
        spectrum = jnp.fft.fft2(current) * lax.complex(wave_cos, wave_sin)
        field_sum = field_sum + 2.0 * jnp.real(jnp.fft.ifft2(spectrum))
    residual = hologram.astype(jnp.float32) - field_sum
    residual_spectrum = jnp.fft.fft2(residual)
    results = []
    for plane_idx in range(PLANES):
        support = support_of(plane_idx)
        current = volume[plane_idx].astype(jnp.float32) * support
        wave_cos, wave_sin = wave_of(plane_idx)
        gradient = 2.0 * jnp.real(jnp.fft.ifft2(residual_spectrum * lax.complex(wave_cos, -wave_sin)))
        updated = current + STEP_SIZE * gradient
        results.append(support * (updated - jnp.clip(updated, -THRESHOLD, THRESHOLD)))
    return jnp.stack(results, axis=0)
```

```python
import math

import jax
import jax.numpy as jnp
import ml_dtypes
import numpy as np
from jax import lax
from jax.experimental import pallas as pl
from jax.experimental.pallas import tpu as pltpu
from jax.sharding import PartitionSpec as P


TILE = 128
N = 4096
ROWS = 64
PLANES = 8
TWO_PI = 2.0 * math.pi
WAVE_RATIO = 0.266
DEPTH_SCALE = 0.001 / 5.32e-07
STEP_SIZE = 0.1
THRESHOLD = 0.25
F32 = jnp.float32
BF16 = jnp.bfloat16
VMEM_LIMIT = 48 * 1024 * 1024


def split_np(table):
    table = np.asarray(table, np.float64)
    high = table.astype(ml_dtypes.bfloat16)
    low = (table - high.astype(np.float64)).astype(ml_dtypes.bfloat16)
    return np.stack([high, low])


def twist_tables():
    k = np.arange(32)[:, None]
    b = np.arange(128)[None, :]
    angle = TWO_PI * ((k * b) % N) / N
    return np.cos(angle).astype(np.float32), np.sin(angle).astype(np.float32)


def matrix_forward():
    b = np.arange(128)
    angle = TWO_PI * ((b[:, None] * b[None, :]) % 128) / 128
    cos, sin = np.cos(angle), np.sin(angle)
    return np.block([[cos, -sin], [sin, cos]])


def matrix_inverse():
    return matrix_forward().T


def matrix_first_slot():
    b = np.arange(128)[:, None]
    m = np.arange(64)[None, :]
    low = TWO_PI * ((b * 32 * m) % N) / N
    high = TWO_PI * ((b * (16 + 32 * m)) % N) / N
    out = np.zeros((256, 256))
    out[:128, :64] = np.cos(low)
    out[:128, 128:192] = -np.sin(low)
    out[:128, 128] = 1.0 - 2.0 * (np.arange(128) % 2)
    out[128:, 64:128] = np.cos(high)
    out[128:, 192:] = -np.sin(high)
    return out


def matrix_first_slot_inverse():
    out = 2.0 * matrix_first_slot().T
    out[0] *= 0.5
    out[128] *= 0.5
    return out


def cosine_coefficients():
    nodes = 0.5 * math.pi**2 * (1.0 - np.cos(np.pi * (np.arange(64) + 0.5) / 64))
    fit = np.polynomial.chebyshev.Chebyshev.fit(nodes, np.cos(np.sqrt(nodes)), 8, domain=[0, math.pi**2])
    return [float(v) for v in fit.convert(kind=np.polynomial.Polynomial).coef]


COSINE = cosine_coefficients()
TURN_HIGH = float(np.float32(math.floor(TWO_PI * 4096) / 4096))
TURN_LOW = TWO_PI - TURN_HIGH


def turned(re, im, index, length, sign):
    index = index % length
    if index == 0:
        return re, im
    if 4 * index == length:
        if im is None:
            return None, (re if sign > 0 else -re)
        return (-im, re) if sign > 0 else (im, -re)
    c = math.cos(TWO_PI * index / length)
    s = sign * math.sin(TWO_PI * index / length)
    if im is None:
        return re * c, re * s
    if 8 * index == length:
        return ((re - im) * c, (re + im) * c) if sign > 0 else ((re + im) * c, (im - re) * c)
    if 8 * index == 3 * length:
        c = -c
        return (-((re + im) * c), (re - im) * c) if sign > 0 else ((im - re) * c, -((re + im) * c))
    return re * c - im * s, re * s + im * c


def plus(a, b):
    return b if a is None else (a if b is None else a + b)


def minus(a, b):
    if b is None:
        return a
    return -b if a is None else a - b


def real_forward(values):
    length = len(values)
    if length == 2:
        return [(values[0] + values[1], None), (values[0] - values[1], None)]
    even = real_forward(values[0::2])
    odd = real_forward(values[1::2])
    out = [None] * (length // 2 + 1)
    for k in range(length // 4 + 1):
        er, ei = even[k]
        tr, ti = turned(odd[k][0], odd[k][1], k, length, -1)
        out[k] = (plus(er, tr), plus(ei, ti))
        if 4 * k != length:
            out[length // 2 - k] = (minus(er, tr), minus(ti, ei))
    return out


def real_inverse(spectrum):
    length = 2 * (len(spectrum) - 1)
    if length == 2:
        return [spectrum[0][0] + spectrum[1][0], spectrum[0][0] - spectrum[1][0]]
    even, odd = [], []
    for k in range(length // 4 + 1):
        zr, zi = spectrum[k]
        yr, yi = spectrum[length // 2 - k]
        if 4 * k == length:
            even.append((zr + zr, None))
            odd.append((-(zi + zi), None))
            continue
        even.append((zr + yr, minus(zi, yi)))
        odd.append(turned(zr - yr, plus(zi, yi), k, length, 1))
    out = [None] * length
    out[0::2] = real_inverse(even)
    out[1::2] = real_inverse(odd)
    return out


def complex_sum(values, sign):
    length = len(values)
    if length == 1:
        return values
    even = complex_sum(values[0::2], sign)
    odd = complex_sum(values[1::2], sign)
    out = [None] * length
    for k in range(length // 2):
        er, ei = even[k]
        tr, ti = turned(odd[k][0], odd[k][1], k, length, sign)
        out[k] = (er + tr, ei + ti)
        out[k + length // 2] = (er - tr, ei - ti)
    return out


def parts(value):
    high = value.astype(BF16)
    return high, (value - high.astype(F32)).astype(BF16)


def mm(a, b, transposed=False):
    dims = (((1,), (1,)), ((), ())) if transposed else (((1,), (0,)), ((), ()))
    return lax.dot_general(a, b, dims, preferred_element_type=F32)


def lanes_of(shape):
    return lax.broadcasted_iota(jnp.int32, shape, len(shape) - 1)


def mark_tiles(tiles_ref, hits_ref, lat_place):
    for t in range(40):
        hits_ref[t] = 0.0
    for slot in range(16):
        hits_ref[tiles_ref[lat_place // 2, slot]] = 1.0


def rows_kernel(ids_ref, tiles_ref, depth_ref, vol_ref, holo_ref, tc_ref, ts_ref, wt_ref, out_ref, cur_ref, y_ref, hits_ref):
    depth_place, lat_place = ids_ref[0], ids_ref[1]
    mark_tiles(tiles_ref, hits_ref, lat_place)
    for a in range(32):
        cols = slice(a * TILE, (a + 1) * TILE)
        cur_ref[0:ROWS, cols] = vol_ref[:, cols].astype(F32) * hits_ref[a]
        cur_ref[ROWS:, cols] = holo_ref[:, cols].astype(F32)

    def group(g, carry):
        row = pl.multiple_of(g * 8, 8)
        base = (g // 8) * 1024 + (g % 8) * 8
        spec = real_forward([cur_ref[pl.ds(row, 8), a * TILE : (a + 1) * TILE] for a in range(32)])
        at = pl.ds(pl.multiple_of(base, 8), 8)
        y_ref[at, :128] = spec[0][0]
        y_ref[at, 128:] = spec[16][0]
        for k in range(1, 16):
            at = pl.ds(pl.multiple_of(base + k * ROWS, 8), 8)
            re, im = spec[k]
            c, s = tc_ref[k : k + 1, :], ts_ref[k : k + 1, :]
            y_ref[at, :128] = re * c + im * s
            y_ref[at, 128:] = im * c - re * s
        return carry

    lax.fori_loop(0, 16, group, 0)

    def apply(start, size, high, low):
        w_high, w_low = wt_ref[0, pl.ds(start, size), :], wt_ref[1, pl.ds(start, size), :]
        return mm(w_high, high, True) + (mm(w_high, low, True) + mm(w_low, high, True))

    for sg in range(4):
        high, low = parts(y_ref[sg * 256 : (sg + 1) * 256, :])
        o = apply(0, 256, high, low)
        for h in range(2):
            part = o[:, h * 128 : (h + 1) * 128]
            if sg == 0 and h == 0:
                first = apply(256, 256, high[:128], low[:128])
                part = jnp.where(lanes_of(part.shape) < ROWS, first, part)
            for c in range(2):
                out_ref[pl.ds(sg * 640 + c * 2 + h, 128, stride=5), :] = part[c * 128 : (c + 1) * 128]

    depth = depth_ref[0]
    half, slot_low = depth_place // 4, depth_place % 4
    for sg in range(4):
        slot = sg * 4 + slot_low
        y = y_ref[pl.ds(pl.multiple_of(1024 + slot * ROWS, ROWS), ROWS), :]
        high, low = parts(jnp.concatenate([y, y], axis=0))
        start = half * 128
        if sg == 0:
            start = start + jnp.where(slot_low == 0, 256, 0)
        o = apply(pl.multiple_of(start, 128), 128, high, low)
        out_ref[pl.ds(sg * 640 + 4, 128, stride=5), :] = jnp.where(lanes_of(o.shape) < ROWS, o, depth)


def signed(index):
    return jnp.where(index < N // 2, index, index - N)


def cosine(angle):
    turns = jnp.round(angle * (1.0 / TWO_PI))
    rest = (angle - turns * TURN_HIGH) - turns * TURN_LOW
    square = rest * rest
    value = COSINE[-1] * square + COSINE[-2]
    for coefficient in COSINE[-3::-1]:
        value = value * square + coefficient
    return value


def columns_kernel(ids_ref, in_ref, tc_ref, ts_ref, w_ref, wi_ref, out_ref, x_ref, z_ref, bend_ref):
    place = ids_ref[0] * ROWS + ids_ref[1]
    first = place == 0
    slot_group, col = place // 128, place % 128
    lane = lanes_of((8, 128))
    left = lane < ROWS
    fourth = lax.broadcasted_iota(jnp.int32, (8, 128), 0) % 4 == 0
    zero = jnp.zeros((8, 128), F32)

    def x_at(g, a, c):
        return pl.ds(pl.multiple_of(g * 512 + a * 16 + c * 8, 8), 8)

    ky = lax.broadcasted_iota(jnp.int32, (32, 128), 0) + 32 * lax.broadcasted_iota(jnp.int32, (32, 128), 1)
    uy = signed(ky).astype(F32) * (WAVE_RATIO / N)
    for g in range(5):
        if g == 4:
            kx = jnp.full((32, 128), -(N // 2), jnp.int32)
        else:
            slot = slot_group * 4 + g
            kx = slot + 32 * col
            if g == 0:
                kx = jnp.where(slot == 0, jnp.where(col < 64, 32 * col, 16 + 32 * (col - 64)), kx)
            kx = signed(jnp.full((32, 128), kx, jnp.int32))
        ux = kx.astype(F32) * (WAVE_RATIO / N)
        squared = uy * uy + ux * ux
        bend_ref[g * 32 : (g + 1) * 32, :] = squared / (1.0 + jnp.sqrt(1.0 - squared))

    depths = in_ref[pl.ds(4, 8, stride=320), :]
    scale = (TWO_PI * DEPTH_SCALE) * jnp.where(left, pltpu.roll(depths, 64, 1), depths)

    def gather(a, carry):
        start = a * 10
        for h in range(2):
            for c in range(2):
                lower = in_ref[pl.ds(start + c * 2 + h, 8, stride=320), :]
                upper = in_ref[pl.ds(start + 5 + c * 2 + h, 8, stride=320), :]
                one = jnp.where(left, lower, pltpu.roll(upper, 64, 1))
                two = jnp.where(left, pltpu.roll(lower, 64, 1), upper)
                if h == 0 and c == 1:
                    x_ref[x_at(5, a, 0), :] = jnp.where(first, one, zero)
                    x_ref[x_at(5, a, 1), :] = zero
                    one = jnp.where(first, zero, one)
                x_ref[x_at(2 * h, a, c), :] = one
                x_ref[x_at(2 * h + 1, a, c), :] = two
        lower = in_ref[pl.ds(start + 4, 8, stride=320), :]
        upper = in_ref[pl.ds(start + 9, 8, stride=320), :]
        both = jnp.where(left, lower, pltpu.roll(upper, 64, 1))
        x_ref[x_at(4, a, 0), :] = both
        x_ref[x_at(4, a, 1), :] = jnp.where(jnp.logical_and(first, fourth), zero, pltpu.roll(both, 4, 0))
        return carry

    lax.fori_loop(0, 32, gather, 0)

    def forward(g, carry):
        values = [(x_ref[x_at(g, a, 0), :], x_ref[x_at(g, a, 1), :]) for a in range(32)]
        for k, (re, im) in enumerate(complex_sum(values, -1)):
            at = pl.ds(pl.multiple_of(g * 256 + k * 8, 8), 8)
            if k > 0:
                c, s = tc_ref[k : k + 1, :], ts_ref[k : k + 1, :]
                re, im = re * c + im * s, im * c - re * s
            z_ref[at, :128] = re
            z_ref[at, 128:] = im
        return carry

    lax.fori_loop(0, 6, forward, 0)

    def product(g, table):
        at = slice(g * 256, (g + 1) * 256)
        high, low = parts(z_ref[at, :])
        z_ref[at, :] = mm(high, table[0]) + (mm(low, table[0]) + mm(high, table[1]))

    for g in range(6):
        product(g, w_ref)

    gain = STEP_SIZE * 2.0 / (N * N)

    def mix(k, carry):
        for index, (g, row) in enumerate(((0, 0), (1, 1), (2, 2), (3, 3), (5, 4))):
            at = pl.ds(pl.multiple_of(g * 256 + k * 8, 8), 8)
            wave = cosine(scale * bend_ref[pl.ds(index * 32 + k, 1), :])
            for half in (slice(0, 128), slice(128, 256)):
                total = jnp.sum(wave * z_ref[at, half], axis=0, keepdims=True)
                observed = z_ref[pl.ds(pl.multiple_of(1024 + k * 8, 8), 8), half]
                residual = observed[row : row + 1] - 2.0 * total
                z_ref[at, half] = (wave * gain) * residual
        return carry

    lax.fori_loop(0, 32, mix, 0)

    for g in (0, 1, 2, 3, 5):
        product(g, wi_ref)

    def backward(g, carry):
        g = jnp.where(g == 4, 5, g)
        values = []
        for k in range(32):
            at = pl.ds(pl.multiple_of(g * 256 + k * 8, 8), 8)
            re, im = z_ref[at, :128], z_ref[at, 128:]
            if k > 0:
                c, s = tc_ref[k : k + 1, :], ts_ref[k : k + 1, :]
                re, im = re * c - im * s, im * c + re * s
            values.append((re, im))
        for a, (re, im) in enumerate(complex_sum(values, 1)):
            x_ref[x_at(g, a, 0), :] = re
            x_ref[x_at(g, a, 1), :] = im
        return carry

    lax.fori_loop(0, 5, backward, 0)

    def scatter(a, carry):
        start = a * 8
        for h in range(2):
            for c in range(2):
                one = x_ref[x_at(2 * h, a, c), :]
                two = x_ref[x_at(2 * h + 1, a, c), :]
                if h == 0 and c == 1:
                    one = jnp.where(first, x_ref[x_at(5, a, 0), :], one)
                lower = jnp.where(left, one, pltpu.roll(two, 64, 1))
                upper = jnp.where(left, pltpu.roll(one, 64, 1), two)
                out_ref[pl.ds(start + c * 2 + h, 8, stride=256), :] = lower
                out_ref[pl.ds(start + 4 + c * 2 + h, 8, stride=256), :] = upper
        return carry

    lax.fori_loop(0, 32, scatter, 0)


def update_kernel(ids_ref, tiles_ref, vol_ref, in_ref, tc_ref, ts_ref, wi_ref, out_ref, y_ref, hits_ref):
    mark_tiles(tiles_ref, hits_ref, ids_ref[1])

    def apply(which, high, low):
        w_high, w_low = wi_ref[0, which], wi_ref[1, which]
        return mm(high, w_high) + (mm(low, w_high) + mm(high, w_low))

    for sg in range(4):
        for h in range(2):
            blocks = [in_ref[pl.ds(sg * 512 + c * 2 + h, 128, stride=4), :].T for c in range(2)]
            high, low = parts(jnp.concatenate(blocks, axis=1))
            slot = sg * 4 + h * 2
            if slot == 0:
                y_ref[0:64, :] = apply(1, high[:64], low[:64])
                y_ref[64:128, :] = apply(0, high[64:], low[64:])
            else:
                y_ref[slot * 64 : slot * 64 + 128, :] = apply(0, high, low)

    def group(g, carry):
        base = g * 8
        at = pl.ds(pl.multiple_of(base, 8), 8)
        spec = [(y_ref[at, :128], None)]
        for k in range(1, 16):
            at = pl.ds(pl.multiple_of(base + k * ROWS, 8), 8)
            re, im = y_ref[at, :128], y_ref[at, 128:]
            c, s = tc_ref[k : k + 1, :], ts_ref[k : k + 1, :]
            spec.append((re * c - im * s, im * c + re * s))
        at = pl.ds(pl.multiple_of(base, 8), 8)
        spec.append((y_ref[at, 128:], None))
        for a, value in enumerate(real_inverse(spec)):
            out_ref[at, a * TILE : (a + 1) * TILE] = value
        return carry

    lax.fori_loop(0, 8, group, 0)
    for a in range(32):
        cols = slice(a * TILE, (a + 1) * TILE)
        support = hits_ref[a]
        updated = vol_ref[:, cols].astype(F32) * support + out_ref[:, cols]
        out_ref[:, cols] = support * (updated - jnp.clip(updated, -THRESHOLD, THRESHOLD))


def call(kernel, out_shape, operands, scalars, scratch):
    specs = [pl.BlockSpec(memory_space=pltpu.SMEM if i < scalars else pltpu.VMEM) for i in range(len(operands))]
    return pl.pallas_call(
        kernel,
        out_shape=jax.ShapeDtypeStruct(out_shape, F32),
        in_specs=specs,
        out_specs=pl.BlockSpec(memory_space=pltpu.VMEM),
        scratch_shapes=scratch,
        compiler_params=pltpu.CompilerParams(vmem_limit_bytes=VMEM_LIMIT),
    )(*operands)


def rows_step(ids, tiles, depth, volume, hologram):
    tc, ts = twist_tables()
    wt = np.concatenate([matrix_forward().T, matrix_first_slot().T], axis=0)
    return call(
        rows_kernel,
        (2560, 128),
        (ids, tiles, depth, volume, hologram, tc, ts, split_np(wt)),
        3,
        [pltpu.VMEM((2 * ROWS, N), F32), pltpu.VMEM((2048, 256), F32), pltpu.SMEM((40,), F32)],
    )


def columns_step(ids, received):
    tc, ts = twist_tables()
    return call(
        columns_kernel,
        (2048, 128),
        (ids, received, tc, ts, split_np(matrix_forward()), split_np(matrix_inverse())),
        1,
        [pltpu.VMEM((3072, 128), F32), pltpu.VMEM((1536, 256), F32), pltpu.VMEM((160, 128), F32)],
    )


def update_step(ids, tiles, volume, received):
    tc, ts = twist_tables()
    wi = split_np(np.stack([matrix_inverse(), matrix_first_slot_inverse()]))
    return call(
        update_kernel,
        (ROWS, N),
        (ids, tiles, volume, received, tc, ts, wi),
        2,
        [pltpu.VMEM((1024, 256), F32), pltpu.SMEM((40,), F32)],
    )


def exchange(value, shape):
    moved = lax.all_to_all(value.reshape(shape), ("depth", "lat"), split_axis=0, concat_axis=0, tiled=True)
    return moved.reshape(value.shape)


def body(volume, hologram, plane_depth, tile_list):
    ids = jnp.stack([lax.axis_index("depth"), lax.axis_index("lat")]).astype(jnp.int32)
    tiles, volume = tile_list[0], volume[0]
    spectra = rows_step(ids, tiles, plane_depth, volume, hologram)
    spectra = exchange(spectra, (512, 1, 640))
    filtered = columns_step(ids, spectra)
    filtered = exchange(filtered, (512, 4, 128))
    return update_step(ids, tiles, volume, filtered)[None]


def solution(mesh):
    return jax.shard_map(
        body,
        mesh=mesh,
        in_specs=(P("depth", "lat", None), P("lat", None), P("depth"), P("depth", None, None)),
        out_specs=P("depth", "lat", None),
        check_vma=False,
    )
```

```python
import math

import jax
import jax.numpy as jnp
import ml_dtypes
import numpy as np
from jax import lax
from jax.experimental import pallas as pl
from jax.experimental.pallas import tpu as pltpu
from jax.sharding import PartitionSpec as P


TILE = 128
N = 4096
ROWS = 64
PLANES = 8
TWO_PI = 2.0 * math.pi
WAVE_RATIO = 0.266
DEPTH_SCALE = 0.001 / 5.32e-07
STEP_SIZE = 0.1
THRESHOLD = 0.25
F32 = jnp.float32
BF16 = jnp.bfloat16
VMEM_LIMIT = 48 * 1024 * 1024
PRODUCT_ROWS = 512


def split_np(table):
    table = np.asarray(table, np.float64)
    high = table.astype(ml_dtypes.bfloat16)
    low = (table - high.astype(np.float64)).astype(ml_dtypes.bfloat16)
    return np.stack([high, low])


def twist_tables():
    k = np.arange(32)[:, None]
    b = np.arange(128)[None, :]
    angle = TWO_PI * ((k * b) % N) / N
    return np.cos(angle).astype(np.float32), np.sin(angle).astype(np.float32)


def matrix_forward():
    b = np.arange(128)
    angle = TWO_PI * ((b[:, None] * b[None, :]) % 128) / 128
    cos, sin = np.cos(angle), np.sin(angle)
    return np.block([[cos, -sin], [sin, cos]])


def matrix_inverse():
    return matrix_forward().T


def matrix_first_slot():
    b = np.arange(128)[:, None]
    m = np.arange(64)[None, :]
    low = TWO_PI * ((b * 32 * m) % N) / N
    high = TWO_PI * ((b * (16 + 32 * m)) % N) / N
    out = np.zeros((256, 256))
    out[:128, :64] = np.cos(low)
    out[:128, 128:192] = -np.sin(low)
    out[:128, 128] = 1.0 - 2.0 * (np.arange(128) % 2)
    out[128:, 64:128] = np.cos(high)
    out[128:, 192:] = -np.sin(high)
    return out


def matrix_first_slot_inverse():
    out = 2.0 * matrix_first_slot().T
    out[0] *= 0.5
    out[128] *= 0.5
    return out


def cosine_coefficients():
    nodes = 0.5 * math.pi**2 * (1.0 - np.cos(np.pi * (np.arange(64) + 0.5) / 64))
    fit = np.polynomial.chebyshev.Chebyshev.fit(nodes, np.cos(np.sqrt(nodes)), 8, domain=[0, math.pi**2])
    return [float(v) for v in fit.convert(kind=np.polynomial.Polynomial).coef]


COSINE = cosine_coefficients()
TURN_HIGH = float(np.float32(math.floor(TWO_PI * 4096) / 4096))
TURN_LOW = TWO_PI - TURN_HIGH


def turned(re, im, index, length, sign):
    index = index % length
    if index == 0:
        return re, im
    if 4 * index == length:
        if im is None:
            return None, (re if sign > 0 else -re)
        return (-im, re) if sign > 0 else (im, -re)
    c = math.cos(TWO_PI * index / length)
    s = sign * math.sin(TWO_PI * index / length)
    if im is None:
        return re * c, re * s
    if 8 * index == length:
        return ((re - im) * c, (re + im) * c) if sign > 0 else ((re + im) * c, (im - re) * c)
    if 8 * index == 3 * length:
        c = -c
        return (-((re + im) * c), (re - im) * c) if sign > 0 else ((im - re) * c, -((re + im) * c))
    return re * c - im * s, re * s + im * c


def plus(a, b):
    return b if a is None else (a if b is None else a + b)


def minus(a, b):
    if b is None:
        return a
    return -b if a is None else a - b


def real_forward(values):
    length = len(values)
    if length == 2:
        return [(values[0] + values[1], None), (values[0] - values[1], None)]
    even = real_forward(values[0::2])
    odd = real_forward(values[1::2])
    out = [None] * (length // 2 + 1)
    for k in range(length // 4 + 1):
        er, ei = even[k]
        tr, ti = turned(odd[k][0], odd[k][1], k, length, -1)
        out[k] = (plus(er, tr), plus(ei, ti))
        if 4 * k != length:
            out[length // 2 - k] = (minus(er, tr), minus(ti, ei))
    return out


def real_inverse(spectrum):
    length = 2 * (len(spectrum) - 1)
    if length == 2:
        return [spectrum[0][0] + spectrum[1][0], spectrum[0][0] - spectrum[1][0]]
    even, odd = [], []
    for k in range(length // 4 + 1):
        zr, zi = spectrum[k]
        yr, yi = spectrum[length // 2 - k]
        if 4 * k == length:
            even.append((zr + zr, None))
            odd.append((-(zi + zi), None))
            continue
        even.append((zr + yr, minus(zi, yi)))
        odd.append(turned(zr - yr, plus(zi, yi), k, length, 1))
    out = [None] * length
    out[0::2] = real_inverse(even)
    out[1::2] = real_inverse(odd)
    return out


def complex_sum(values, sign):
    length = len(values)
    if length == 1:
        return values
    even = complex_sum(values[0::2], sign)
    odd = complex_sum(values[1::2], sign)
    out = [None] * length
    for k in range(length // 2):
        er, ei = even[k]
        tr, ti = turned(odd[k][0], odd[k][1], k, length, sign)
        out[k] = (er + tr, ei + ti)
        out[k + length // 2] = (er - tr, ei - ti)
    return out


def parts(value):
    high = value.astype(BF16)
    return high, (value - high.astype(F32)).astype(BF16)


def mm(a, b, transposed=False):
    dims = (((1,), (1,)), ((), ())) if transposed else (((1,), (0,)), ((), ()))
    return lax.dot_general(a, b, dims, preferred_element_type=F32)


def lanes_of(shape):
    return lax.broadcasted_iota(jnp.int32, shape, len(shape) - 1)


def mark_tiles(tiles_ref, hits_ref, lat_place):
    for t in range(40):
        hits_ref[t] = 0.0
    for slot in range(16):
        hits_ref[tiles_ref[slot, lat_place // 2]] = 1.0


def rows_kernel(ids_ref, tiles_ref, depth_ref, vol_ref, holo_ref, tw_ref, wt_hbm, out_ref, src_ref, tw, wt_ref, y_ref, hits_ref, sems):
    copies = [
        pltpu.make_async_copy(vol_ref, src_ref.at[0:ROWS], sems.at[0]),
        pltpu.make_async_copy(holo_ref, src_ref.at[ROWS : 2 * ROWS], sems.at[1]),
        pltpu.make_async_copy(tw_ref, tw, sems.at[2]),
        pltpu.make_async_copy(wt_hbm, wt_ref, sems.at[3]),
    ]
    for copy in copies:
        copy.start()
    depth_place, lat_place = ids_ref[0], ids_ref[1]
    mark_tiles(tiles_ref, hits_ref, lat_place)
    for a in range(32):
        hits_ref[40 + a] = 1.0
    for copy in copies[:3]:
        copy.wait()

    def group(g, carry):
        which = g // 4
        values = []
        for a in range(32):
            tile = src_ref[pl.ds(pl.multiple_of(g * 16, 16), 16), a * TILE : (a + 1) * TILE]
            values.append(tile.astype(F32) * hits_ref[which * 40 + a])
        base = which * 1024 + (g % 4) * 16
        spec = real_forward(values)
        at = pl.ds(pl.multiple_of(base, 16), 16)
        y_ref[at, :128] = spec[0][0]
        y_ref[at, 128:] = spec[16][0]
        for k in range(1, 16):
            at = pl.ds(pl.multiple_of(base + k * ROWS, 16), 16)
            re, im = spec[k]
            c, s = tw[k : k + 1, :], tw[32 + k : 33 + k, :]
            y_ref[at, :128] = re * c + im * s
            y_ref[at, 128:] = im * c - re * s
        return carry

    lax.fori_loop(0, 8, group, 0)
    copies[3].wait()

    def apply(start, size, high, low):
        w_high, w_low = wt_ref[0, pl.ds(start, size), :], wt_ref[1, pl.ds(start, size), :]
        return mm(w_high, high, True) + (mm(w_high, low, True) + mm(w_low, high, True))

    for sg in range(4):
        high, low = parts(y_ref[sg * 256 : (sg + 1) * 256, :])
        o = apply(0, 256, high, low)
        for h in range(2):
            part = o[:, h * 128 : (h + 1) * 128]
            if sg == 0 and h == 0:
                first = apply(256, 256, high[:128], low[:128])
                part = jnp.where(lanes_of(part.shape) < ROWS, first, part)
            for c in range(2):
                out_ref[pl.ds(sg * 640 + c * 2 + h, 128, stride=5), :] = part[c * 128 : (c + 1) * 128]

    depth = depth_ref[0]
    half, slot_low = depth_place // 4, depth_place % 4
    for sg in range(4):
        slot = sg * 4 + slot_low
        y = y_ref[pl.ds(pl.multiple_of(1024 + slot * ROWS, ROWS), ROWS), :]
        high, low = parts(jnp.concatenate([y, y], axis=0))
        start = half * 128
        if sg == 0:
            start = start + jnp.where(slot_low == 0, 256, 0)
        o = apply(pl.multiple_of(start, 128), 128, high, low)
        out_ref[pl.ds(sg * 640 + 4, 128, stride=5), :] = jnp.where(lanes_of(o.shape) < ROWS, o, depth)


def signed(index):
    return jnp.where(index < N // 2, index, index - N)


def cosine(angle):
    turns = jnp.round(angle * (1.0 / TWO_PI))
    rest = (angle - turns * TURN_HIGH) - turns * TURN_LOW
    square = rest * rest
    value = COSINE[-1] * square + COSINE[-2]
    for coefficient in COSINE[-3::-1]:
        value = value * square + coefficient
    return value


def columns_kernel(ids_ref, in_ref, tc_ref, ts_ref, w_ref, wi_ref, out_ref, x_ref, zr_ref, zi_ref, bend_ref):
    place = ids_ref[1] * PLANES + ids_ref[0]
    first = place == 0
    slot_group, col = place // 128, place % 128
    left = lanes_of((8, 128)) < ROWS
    fourth = lax.broadcasted_iota(jnp.int32, (8, 128), 0) % 4 == 0
    zero = jnp.zeros((8, 128), F32)

    def swap(value):
        return pltpu.roll(value, ROWS, 1)

    def x_at(g, a, c):
        return pl.ds(pl.multiple_of(g * 512 + a * 16 + c * 8, 8), 8)

    def received(a, upper, q):
        return in_ref[pl.ds(a * 80 + upper * 40 + q, 8, stride=5), :]

    def store_spectrum(g, k, re, im):
        if k > 0:
            c, s = tc_ref[k : k + 1, :], ts_ref[k : k + 1, :]
            re, im = re * c + im * s, im * c - re * s
        at = pl.ds(g * 320 + k, 8, stride=40)
        zr_ref[at, :] = re
        zi_ref[at, :] = im

    ky = lax.broadcasted_iota(jnp.int32, (32, 128), 0) + 32 * lax.broadcasted_iota(jnp.int32, (32, 128), 1)
    uy = signed(ky).astype(F32) * (WAVE_RATIO / N)
    for g in range(5):
        if g == 4:
            kx = jnp.full((32, 128), -(N // 2), jnp.int32)
        else:
            slot = slot_group * 4 + g
            kx = slot + 32 * col
            if g == 0:
                kx = jnp.where(slot == 0, jnp.where(col < 64, 32 * col, 16 + 32 * (col - 64)), kx)
            kx = signed(jnp.full((32, 128), kx, jnp.int32))
        ux = kx.astype(F32) * (WAVE_RATIO / N)
        squared = uy * uy + ux * ux
        bend_ref[g * 32 : (g + 1) * 32, :] = squared / (1.0 + jnp.sqrt(1.0 - squared))

    def forward(h, carry):
        packed = jnp.logical_and(jnp.logical_and(first, h == 0), left)
        halves = []
        for upper in range(2):
            values = []
            for a in range(32):
                re, im = received(a, upper, h), received(a, upper, 2 + h)
                values.append((re, jnp.where(packed, zero, im)))
            halves.append(complex_sum(values, -1))
        for k in range(32):
            lower, upper = halves[0][k], halves[1][k]
            store_spectrum(2 * h, k, *[jnp.where(left, p, swap(q)) for p, q in zip(lower, upper)])
            store_spectrum(2 * h + 1, k, *[jnp.where(left, swap(p), q) for p, q in zip(lower, upper)])
        return carry

    lax.fori_loop(0, 2, forward, 0)

    def gather(a, carry):
        both = jnp.where(left, received(a, 0, 4), swap(received(a, 1, 4)))
        x_ref[x_at(0, a, 0), :] = both
        x_ref[x_at(0, a, 1), :] = jnp.where(jnp.logical_and(first, fourth), zero, pltpu.roll(both, 4, 0))
        both = jnp.where(left, received(a, 0, 2), swap(received(a, 1, 2)))
        x_ref[x_at(1, a, 0), :] = jnp.where(first, both, zero)
        x_ref[x_at(1, a, 1), :] = zero
        return carry

    lax.fori_loop(0, 32, gather, 0, unroll=8)

    def forward_extra(g, carry):
        values = [(x_ref[x_at(g, a, 0), :], x_ref[x_at(g, a, 1), :]) for a in range(32)]
        for k, (re, im) in enumerate(complex_sum(values, -1)):
            store_spectrum(4 + g, k, re, im)
        return carry

    lax.fori_loop(0, 2, forward_extra, 0)

    def product(start, size, table):
        slabs = [slice((r // 32) * 40, (r // 32) * 40 + 32) for r in range(start, start + size, 32)]
        pairs = [parts(jnp.concatenate([ref[at, :] for at in slabs], axis=0)) for ref in (zr_ref, zi_ref)]
        high = jnp.concatenate([pairs[0][0], pairs[1][0]], axis=1)
        low = jnp.concatenate([pairs[0][1], pairs[1][1]], axis=1)
        value = mm(high, table[0]) + (mm(low, table[0]) + mm(high, table[1]))
        for i, at in enumerate(slabs):
            zr_ref[at, :] = value[i * 32 : (i + 1) * 32, :128]
            zi_ref[at, :] = value[i * 32 : (i + 1) * 32, 128:]

    for start in range(0, 1536, PRODUCT_ROWS):
        product(start, PRODUCT_ROWS, w_ref)

    scales = []
    for p in range(PLANES):
        row = jnp.broadcast_to(in_ref[p * 5 + 4 : p * 5 + 5, :], (8, 128))
        scales.append((TWO_PI * DEPTH_SCALE) * jnp.where(left, swap(row), row))
    gain = STEP_SIZE * 2.0 / (N * N)

    def mix(j, carry):
        extra = None
        for index, g in ((4, 5), (0, 0), (1, 1), (2, 2), (3, 3)):
            bend = bend_ref[pl.ds(pl.multiple_of(index * 32 + j * 8, 8), 8), :]
            waves = [cosine(scale * bend) for scale in scales]
            rows = [pl.ds(pl.multiple_of(g * 320 + p * 40 + j * 8, 8), 8) for p in range(PLANES)]
            at = pl.ds(pl.multiple_of(1280 + index * 40 + j * 8, 8), 8)
            scaled = []
            for ref in (zr_ref, zi_ref):
                terms = [wave * ref[row, :] for wave, row in zip(waves, rows)]
                while len(terms) > 1:
                    terms = [p + q for p, q in zip(terms[0::2], terms[1::2])]
                scaled.append((ref[at, :] - 2.0 * terms[0]) * gain)
            if index == 4:
                extra = [jnp.where(first, value, zero) for value in scaled], waves
                continue
            for p, row in enumerate(rows):
                re, im = waves[p] * scaled[0], waves[p] * scaled[1]
                if index == 0:
                    re = re - extra[1][p] * extra[0][1]
                    im = im + extra[1][p] * extra[0][0]
                zr_ref[row, :] = re
                zi_ref[row, :] = im
        return carry

    lax.fori_loop(0, 4, mix, 0)

    for start in range(0, 1024, PRODUCT_ROWS):
        product(start, PRODUCT_ROWS, wi_ref)

    def backward(h, carry):
        lower, upper = [], []
        for k in range(32):
            columns = []
            for g in (2 * h, 2 * h + 1):
                at = pl.ds(g * 320 + k, 8, stride=40)
                re, im = zr_ref[at, :], zi_ref[at, :]
                if k > 0:
                    c, s = tc_ref[k : k + 1, :], ts_ref[k : k + 1, :]
                    re, im = re * c - im * s, im * c + re * s
                columns.append((re, im))
            lower.append(tuple(jnp.where(left, p, swap(q)) for p, q in zip(*columns)))
            upper.append(tuple(jnp.where(left, swap(p), q) for p, q in zip(*columns)))
        for number, values in enumerate((lower, upper)):
            for a, (re, im) in enumerate(complex_sum(values, 1)):
                out_ref[pl.ds(a * 64 + number * 32 + h, 8, stride=4), :] = re
                out_ref[pl.ds(a * 64 + number * 32 + 2 + h, 8, stride=4), :] = im
        return carry

    lax.fori_loop(0, 2, backward, 0)


def update_kernel(ids_ref, tiles_ref, vol_ref, in_ref, tc_ref, ts_ref, wi_ref, out_ref, y_ref, hits_ref):
    mark_tiles(tiles_ref, hits_ref, ids_ref[1])

    def apply(which, high, low):
        w_high, w_low = wi_ref[0, which], wi_ref[1, which]
        return mm(high, w_high) + (mm(low, w_high) + mm(high, w_low))

    for sg in range(4):
        for h in range(2):
            blocks = [in_ref[pl.ds(sg * 512 + c * 2 + h, 128, stride=4), :].T for c in range(2)]
            high, low = parts(jnp.concatenate(blocks, axis=1))
            slot = sg * 4 + h * 2
            if slot == 0:
                y_ref[0:64, :] = apply(1, high[:64], low[:64])
                y_ref[64:128, :] = apply(0, high[64:], low[64:])
            else:
                y_ref[slot * 64 : slot * 64 + 128, :] = apply(0, high, low)

    def group(g, carry):
        base = g * 8
        at = pl.ds(pl.multiple_of(base, 8), 8)
        spec = [(y_ref[at, :128], None)]
        for k in range(1, 16):
            at = pl.ds(pl.multiple_of(base + k * ROWS, 8), 8)
            re, im = y_ref[at, :128], y_ref[at, 128:]
            c, s = tc_ref[k : k + 1, :], ts_ref[k : k + 1, :]
            spec.append((re * c - im * s, im * c + re * s))
        at = pl.ds(pl.multiple_of(base, 8), 8)
        spec.append((y_ref[at, 128:], None))
        for a, value in enumerate(real_inverse(spec)):
            out_ref[at, a * TILE : (a + 1) * TILE] = value
        return carry

    lax.fori_loop(0, 8, group, 0)
    for a in range(32):
        cols = slice(a * TILE, (a + 1) * TILE)
        support = hits_ref[a]
        updated = vol_ref[:, cols].astype(F32) * support + out_ref[:, cols]
        out_ref[:, cols] = support * (updated - jnp.clip(updated, -THRESHOLD, THRESHOLD))


def call(kernel, out_shape, operands, places, scratch):
    spaces = {"s": pltpu.SMEM, "v": pltpu.VMEM, "h": pltpu.HBM}
    return pl.pallas_call(
        kernel,
        out_shape=jax.ShapeDtypeStruct(out_shape, F32),
        in_specs=[pl.BlockSpec(memory_space=spaces[place]) for place in places],
        out_specs=pl.BlockSpec(memory_space=pltpu.VMEM),
        scratch_shapes=scratch,
        compiler_params=pltpu.CompilerParams(vmem_limit_bytes=VMEM_LIMIT),
    )(*operands)


def rows_step(ids, tiles, depth, volume, hologram):
    wt = np.concatenate([matrix_forward().T, matrix_first_slot().T], axis=0)
    return call(
        rows_kernel,
        (2560, 128),
        (ids, tiles, depth, volume, hologram, np.concatenate(twist_tables()), split_np(wt)),
        "ssshhhh",
        [
            pltpu.VMEM((2 * ROWS, N), BF16),
            pltpu.VMEM((64, 128), F32),
            pltpu.VMEM((2, 512, 256), BF16),
            pltpu.VMEM((2048, 256), F32),
            pltpu.SMEM((80,), F32),
            pltpu.SemaphoreType.DMA((4,)),
        ],
    )


def columns_step(ids, received):
    tc, ts = twist_tables()
    return call(
        columns_kernel,
        (2048, 128),
        (ids, received, tc, ts, split_np(matrix_forward()), split_np(matrix_inverse())),
        "svvvvv",
        [
            pltpu.VMEM((1024, 128), F32),
            pltpu.VMEM((1920, 128), F32),
            pltpu.VMEM((1920, 128), F32),
            pltpu.VMEM((160, 128), F32),
        ],
    )


def update_step(ids, tiles, volume, received):
    tc, ts = twist_tables()
    wi = split_np(np.stack([matrix_inverse(), matrix_first_slot_inverse()]))
    return call(
        update_kernel,
        (ROWS, N),
        (ids, tiles, volume, received, tc, ts, wi),
        "ssvvvvv",
        [pltpu.VMEM((1024, 256), F32), pltpu.SMEM((40,), F32)],
    )


def exchange(value, shape):
    moved = lax.all_to_all(value.reshape(shape), ("lat", "depth"), split_axis=0, concat_axis=0, tiled=True)
    return moved.reshape(value.shape)


def body(volume, hologram, plane_depth, tile_list):
    ids = jnp.stack([lax.axis_index("depth"), lax.axis_index("lat")]).astype(jnp.int32)
    tiles, volume = tile_list[0].T, volume[0]
    spectra = rows_step(ids, tiles, plane_depth, volume, hologram)
    spectra = exchange(spectra, (512, 1, 640))
    filtered = columns_step(ids, spectra)
    filtered = exchange(filtered, (512, 4, 128))
    return update_step(ids, tiles, volume, filtered)[None]


def solution(mesh):
    return jax.shard_map(
        body,
        mesh=mesh,
        in_specs=(P("depth", "lat", None), P("lat", None), P("depth"), P("depth", None, None)),
        out_specs=P("depth", "lat", None),
        check_vma=False,
    )
```

```python
import math

import jax
import jax.numpy as jnp
import ml_dtypes
import numpy as np
from jax import lax
from jax.experimental import pallas as pl
from jax.experimental.pallas import tpu as pltpu
from jax.sharding import PartitionSpec as P


TILE = 128
N = 4096
ROWS = 64
PLANES = 8
TWO_PI = 2.0 * math.pi
WAVE_RATIO = 0.266
DEPTH_SCALE = 0.001 / 5.32e-07
STEP_SIZE = 0.1
THRESHOLD = 0.25
F32 = jnp.float32
BF16 = jnp.bfloat16
VMEM_LIMIT = 48 * 1024 * 1024
PRODUCT_ROWS = 512


def split_np(table):
    table = np.asarray(table, np.float64)
    high = table.astype(ml_dtypes.bfloat16)
    low = (table - high.astype(np.float64)).astype(ml_dtypes.bfloat16)
    return np.stack([high, low])


def twist_tables():
    k = np.arange(32)[:, None]
    b = np.arange(128)[None, :]
    angle = TWO_PI * ((k * b) % N) / N
    return np.cos(angle).astype(np.float32), np.sin(angle).astype(np.float32)


def matrix_forward():
    b = np.arange(128)
    angle = TWO_PI * ((b[:, None] * b[None, :]) % 128) / 128
    cos, sin = np.cos(angle), np.sin(angle)
    return np.block([[cos, -sin], [sin, cos]])


def matrix_inverse():
    return matrix_forward().T


def matrix_first_slot():
    b = np.arange(128)[:, None]
    m = np.arange(64)[None, :]
    low = TWO_PI * ((b * 32 * m) % N) / N
    high = TWO_PI * ((b * (16 + 32 * m)) % N) / N
    out = np.zeros((256, 256))
    out[:128, :64] = np.cos(low)
    out[:128, 128:192] = -np.sin(low)
    out[:128, 128] = 1.0 - 2.0 * (np.arange(128) % 2)
    out[128:, 64:128] = np.cos(high)
    out[128:, 192:] = -np.sin(high)
    return out


def matrix_first_slot_inverse():
    out = 2.0 * matrix_first_slot().T
    out[0] *= 0.5
    out[128] *= 0.5
    return out


def cosine_coefficients():
    nodes = 0.5 * math.pi**2 * (1.0 - np.cos(np.pi * (np.arange(64) + 0.5) / 64))
    fit = np.polynomial.chebyshev.Chebyshev.fit(nodes, np.cos(np.sqrt(nodes)), 8, domain=[0, math.pi**2])
    return [float(v) for v in fit.convert(kind=np.polynomial.Polynomial).coef]


COSINE = cosine_coefficients()
TURN_HIGH = float(np.float32(math.floor(TWO_PI * 4096) / 4096))
TURN_LOW = TWO_PI - TURN_HIGH


def turned(re, im, index, length, sign):
    index = index % length
    if index == 0:
        return re, im
    if 4 * index == length:
        if im is None:
            return None, (re if sign > 0 else -re)
        return (-im, re) if sign > 0 else (im, -re)
    c = math.cos(TWO_PI * index / length)
    s = sign * math.sin(TWO_PI * index / length)
    if im is None:
        return re * c, re * s
    if 8 * index == length:
        return ((re - im) * c, (re + im) * c) if sign > 0 else ((re + im) * c, (im - re) * c)
    if 8 * index == 3 * length:
        c = -c
        return (-((re + im) * c), (re - im) * c) if sign > 0 else ((im - re) * c, -((re + im) * c))
    return re * c - im * s, re * s + im * c


def plus(a, b):
    return b if a is None else (a if b is None else a + b)


def minus(a, b):
    if b is None:
        return a
    return -b if a is None else a - b


def real_forward(values):
    length = len(values)
    if length == 2:
        return [(values[0] + values[1], None), (values[0] - values[1], None)]
    even = real_forward(values[0::2])
    odd = real_forward(values[1::2])
    out = [None] * (length // 2 + 1)
    for k in range(length // 4 + 1):
        er, ei = even[k]
        tr, ti = turned(odd[k][0], odd[k][1], k, length, -1)
        out[k] = (plus(er, tr), plus(ei, ti))
        if 4 * k != length:
            out[length // 2 - k] = (minus(er, tr), minus(ti, ei))
    return out


def real_inverse(spectrum):
    length = 2 * (len(spectrum) - 1)
    if length == 2:
        return [spectrum[0][0] + spectrum[1][0], spectrum[0][0] - spectrum[1][0]]
    even, odd = [], []
    for k in range(length // 4 + 1):
        zr, zi = spectrum[k]
        yr, yi = spectrum[length // 2 - k]
        if 4 * k == length:
            even.append((zr + zr, None))
            odd.append((-(zi + zi), None))
            continue
        even.append((zr + yr, minus(zi, yi)))
        odd.append(turned(zr - yr, plus(zi, yi), k, length, 1))
    out = [None] * length
    out[0::2] = real_inverse(even)
    out[1::2] = real_inverse(odd)
    return out


def complex_sum(values, sign):
    length = len(values)
    if length == 1:
        return values
    even = complex_sum(values[0::2], sign)
    odd = complex_sum(values[1::2], sign)
    out = [None] * length
    for k in range(length // 2):
        er, ei = even[k]
        tr, ti = turned(odd[k][0], odd[k][1], k, length, sign)
        out[k] = (er + tr, ei + ti)
        out[k + length // 2] = (er - tr, ei - ti)
    return out


def parts(value):
    high = value.astype(BF16)
    return high, (value - high.astype(F32)).astype(BF16)


def mm(a, b, transposed=False):
    dims = (((1,), (1,)), ((), ())) if transposed else (((1,), (0,)), ((), ()))
    return lax.dot_general(a, b, dims, preferred_element_type=F32)


def lanes_of(shape):
    return lax.broadcasted_iota(jnp.int32, shape, len(shape) - 1)


def places():
    return lax.axis_index("depth"), lax.axis_index("lat")


def mark_tiles(tiles_ref, hits_ref, lat_place):
    for t in range(40):
        hits_ref[t] = 0.0
    for slot in range(16):
        hits_ref[tiles_ref[slot, lat_place // 2]] = 1.0


def rows_kernel(
    depth_ref, tiles_hbm, vol_hbm, holo_hbm, tw_hbm, wt_hbm, out_ref, tiles_ref, src_ref, tw, wt_ref, y_ref, hits_ref, sems
):
    copies = [
        pltpu.make_async_copy(tiles_hbm, tiles_ref, sems.at[4]),
        pltpu.make_async_copy(vol_hbm, src_ref.at[0:ROWS], sems.at[0]),
        pltpu.make_async_copy(holo_hbm, src_ref.at[ROWS : 2 * ROWS], sems.at[1]),
        pltpu.make_async_copy(tw_hbm, tw, sems.at[2]),
        pltpu.make_async_copy(wt_hbm, wt_ref, sems.at[3]),
    ]
    for copy in copies:
        copy.start()
    depth_place, lat_place = places()
    for a in range(32):
        hits_ref[40 + a] = 1.0
    copies[0].wait()
    mark_tiles(tiles_ref, hits_ref, lat_place)
    for copy in copies[1:4]:
        copy.wait()

    def group(g, carry):
        which = g // 4
        values = []
        for a in range(32):
            tile = src_ref[pl.ds(pl.multiple_of(g * 16, 16), 16), a * TILE : (a + 1) * TILE]
            values.append(tile.astype(F32) * hits_ref[which * 40 + a])
        base = which * 1024 + (g % 4) * 16
        spec = real_forward(values)
        at = pl.ds(pl.multiple_of(base, 16), 16)
        y_ref[at, :128] = spec[0][0]
        y_ref[at, 128:] = spec[16][0]
        for k in range(1, 16):
            at = pl.ds(pl.multiple_of(base + k * ROWS, 16), 16)
            re, im = spec[k]
            c, s = tw[k : k + 1, :], tw[32 + k : 33 + k, :]
            y_ref[at, :128] = re * c + im * s
            y_ref[at, 128:] = im * c - re * s
        return carry

    lax.fori_loop(0, 8, group, 0)
    copies[4].wait()

    def apply(start, size, high, low):
        w_high, w_low = wt_ref[0, pl.ds(start, size), :], wt_ref[1, pl.ds(start, size), :]
        return mm(w_high, high, True) + (mm(w_high, low, True) + mm(w_low, high, True))

    for sg in range(4):
        high, low = parts(y_ref[sg * 256 : (sg + 1) * 256, :])
        o = apply(0, 256, high, low)
        for h in range(2):
            part = o[:, h * 128 : (h + 1) * 128]
            if sg == 0 and h == 0:
                first = apply(256, 256, high[:128], low[:128])
                part = jnp.where(lanes_of(part.shape) < ROWS, first, part)
            for c in range(2):
                out_ref[pl.ds(sg * 640 + c * 2 + h, 128, stride=5), :] = part[c * 128 : (c + 1) * 128]

    depth = depth_ref[0]
    half, slot_low = depth_place // 4, depth_place % 4
    for sg in range(4):
        slot = sg * 4 + slot_low
        y = y_ref[pl.ds(pl.multiple_of(1024 + slot * ROWS, ROWS), ROWS), :]
        high, low = parts(jnp.concatenate([y, y], axis=0))
        start = half * 128
        if sg == 0:
            start = start + jnp.where(slot_low == 0, 256, 0)
        o = apply(pl.multiple_of(start, 128), 128, high, low)
        out_ref[pl.ds(sg * 640 + 4, 128, stride=5), :] = jnp.where(lanes_of(o.shape) < ROWS, o, depth)


def signed(index):
    return jnp.where(index < N // 2, index, index - N)


def cosine(angle):
    turns = jnp.round(angle * (1.0 / TWO_PI))
    rest = (angle - turns * TURN_HIGH) - turns * TURN_LOW
    square = rest * rest
    value = COSINE[-1] * square + COSINE[-2]
    for coefficient in COSINE[-3::-1]:
        value = value * square + coefficient
    return value


def columns_kernel(in_ref, tc_ref, ts_ref, w_ref, wi_ref, out_ref, x_ref, zr_ref, zi_ref, bend_ref):
    depth_place, lat_place = places()
    place = lat_place * PLANES + depth_place
    first = place == 0
    slot_group, col = place // 128, place % 128
    left = lanes_of((8, 128)) < ROWS
    fourth = lax.broadcasted_iota(jnp.int32, (8, 128), 0) % 4 == 0
    zero = jnp.zeros((8, 128), F32)

    def swap(value):
        return pltpu.roll(value, ROWS, 1)

    def x_at(g, a, c):
        return pl.ds(pl.multiple_of(g * 512 + a * 16 + c * 8, 8), 8)

    def received(a, upper, q):
        return in_ref[pl.ds(a * 80 + upper * 40 + q, 8, stride=5), :]

    def store_spectrum(g, k, re, im):
        if k > 0:
            c, s = tc_ref[k : k + 1, :], ts_ref[k : k + 1, :]
            re, im = re * c + im * s, im * c - re * s
        at = pl.ds(g * 320 + k, 8, stride=40)
        zr_ref[at, :] = re
        zi_ref[at, :] = im

    ky = lax.broadcasted_iota(jnp.int32, (32, 128), 0) + 32 * lax.broadcasted_iota(jnp.int32, (32, 128), 1)
    uy = signed(ky).astype(F32) * (WAVE_RATIO / N)
    for g in range(5):
        if g == 4:
            kx = jnp.full((32, 128), -(N // 2), jnp.int32)
        else:
            slot = slot_group * 4 + g
            kx = slot + 32 * col
            if g == 0:
                kx = jnp.where(slot == 0, jnp.where(col < 64, 32 * col, 16 + 32 * (col - 64)), kx)
            kx = signed(jnp.full((32, 128), kx, jnp.int32))
        ux = kx.astype(F32) * (WAVE_RATIO / N)
        squared = uy * uy + ux * ux
        bend_ref[g * 32 : (g + 1) * 32, :] = squared / (1.0 + jnp.sqrt(1.0 - squared))

    def forward(h, carry):
        packed = jnp.logical_and(jnp.logical_and(first, h == 0), left)
        halves = []
        for upper in range(2):
            values = []
            for a in range(32):
                re, im = received(a, upper, h), received(a, upper, 2 + h)
                values.append((re, jnp.where(packed, zero, im)))
            halves.append(complex_sum(values, -1))
        for k in range(32):
            lower, upper = halves[0][k], halves[1][k]
            store_spectrum(2 * h, k, *[jnp.where(left, p, swap(q)) for p, q in zip(lower, upper)])
            store_spectrum(2 * h + 1, k, *[jnp.where(left, swap(p), q) for p, q in zip(lower, upper)])
        return carry

    lax.fori_loop(0, 2, forward, 0)

    def gather(a, carry):
        both = jnp.where(left, received(a, 0, 4), swap(received(a, 1, 4)))
        x_ref[x_at(0, a, 0), :] = both
        x_ref[x_at(0, a, 1), :] = jnp.where(jnp.logical_and(first, fourth), zero, pltpu.roll(both, 4, 0))
        both = jnp.where(left, received(a, 0, 2), swap(received(a, 1, 2)))
        x_ref[x_at(1, a, 0), :] = jnp.where(first, both, zero)
        x_ref[x_at(1, a, 1), :] = zero
        return carry

    lax.fori_loop(0, 32, gather, 0, unroll=8)

    def forward_extra(g, carry):
        values = [(x_ref[x_at(g, a, 0), :], x_ref[x_at(g, a, 1), :]) for a in range(32)]
        for k, (re, im) in enumerate(complex_sum(values, -1)):
            store_spectrum(4 + g, k, re, im)
        return carry

    lax.fori_loop(0, 2, forward_extra, 0)

    def product(start, size, table):
        slabs = [slice((r // 32) * 40, (r // 32) * 40 + 32) for r in range(start, start + size, 32)]
        pairs = [parts(jnp.concatenate([ref[at, :] for at in slabs], axis=0)) for ref in (zr_ref, zi_ref)]
        high = jnp.concatenate([pairs[0][0], pairs[1][0]], axis=1)
        low = jnp.concatenate([pairs[0][1], pairs[1][1]], axis=1)
        value = mm(high, table[0]) + (mm(low, table[0]) + mm(high, table[1]))
        for i, at in enumerate(slabs):
            zr_ref[at, :] = value[i * 32 : (i + 1) * 32, :128]
            zi_ref[at, :] = value[i * 32 : (i + 1) * 32, 128:]

    for start in range(0, 1536, PRODUCT_ROWS):
        product(start, PRODUCT_ROWS, w_ref)

    scales = []
    for p in range(PLANES):
        row = jnp.broadcast_to(in_ref[p * 5 + 4 : p * 5 + 5, :], (8, 128))
        scales.append((TWO_PI * DEPTH_SCALE) * jnp.where(left, swap(row), row))
    gain = STEP_SIZE * 2.0 / (N * N)

    def mix(j, carry):
        extra = None
        for index, g in ((4, 5), (0, 0), (1, 1), (2, 2), (3, 3)):
            bend = bend_ref[pl.ds(pl.multiple_of(index * 32 + j * 8, 8), 8), :]
            waves = [cosine(scale * bend) for scale in scales]
            rows = [pl.ds(pl.multiple_of(g * 320 + p * 40 + j * 8, 8), 8) for p in range(PLANES)]
            at = pl.ds(pl.multiple_of(1280 + index * 40 + j * 8, 8), 8)
            scaled = []
            for ref in (zr_ref, zi_ref):
                terms = [wave * ref[row, :] for wave, row in zip(waves, rows)]
                while len(terms) > 1:
                    terms = [p + q for p, q in zip(terms[0::2], terms[1::2])]
                scaled.append((ref[at, :] - 2.0 * terms[0]) * gain)
            if index == 4:
                extra = [jnp.where(first, value, zero) for value in scaled], waves
                continue
            for p, row in enumerate(rows):
                re, im = waves[p] * scaled[0], waves[p] * scaled[1]
                if index == 0:
                    re = re - extra[1][p] * extra[0][1]
                    im = im + extra[1][p] * extra[0][0]
                zr_ref[row, :] = re
                zi_ref[row, :] = im
        return carry

    lax.fori_loop(0, 4, mix, 0)

    for start in range(0, 1024, PRODUCT_ROWS):
        product(start, PRODUCT_ROWS, wi_ref)

    def backward(h, carry):
        lower, upper = [], []
        for k in range(32):
            columns = []
            for g in (2 * h, 2 * h + 1):
                at = pl.ds(g * 320 + k, 8, stride=40)
                re, im = zr_ref[at, :], zi_ref[at, :]
                if k > 0:
                    c, s = tc_ref[k : k + 1, :], ts_ref[k : k + 1, :]
                    re, im = re * c - im * s, im * c + re * s
                columns.append((re, im))
            lower.append(tuple(jnp.where(left, p, swap(q)) for p, q in zip(*columns)))
            upper.append(tuple(jnp.where(left, swap(p), q) for p, q in zip(*columns)))
        for number, values in enumerate((lower, upper)):
            for a, (re, im) in enumerate(complex_sum(values, 1)):
                out_ref[pl.ds(a * 64 + number * 32 + h, 8, stride=4), :] = re
                out_ref[pl.ds(a * 64 + number * 32 + 2 + h, 8, stride=4), :] = im
        return carry

    lax.fori_loop(0, 2, backward, 0)


def update_kernel(tiles_ref, vol_ref, in_ref, tc_ref, ts_ref, wi_ref, out_ref, y_ref, hits_ref):
    mark_tiles(tiles_ref, hits_ref, places()[1])

    def apply(which, high, low):
        w_high, w_low = wi_ref[0, which], wi_ref[1, which]
        return mm(high, w_high) + (mm(low, w_high) + mm(high, w_low))

    for sg in range(4):
        for h in range(2):
            blocks = [in_ref[pl.ds(sg * 512 + c * 2 + h, 128, stride=4), :].T for c in range(2)]
            high, low = parts(jnp.concatenate(blocks, axis=1))
            slot = sg * 4 + h * 2
            if slot == 0:
                y_ref[0:64, :] = apply(1, high[:64], low[:64])
                y_ref[64:128, :] = apply(0, high[64:], low[64:])
            else:
                y_ref[slot * 64 : slot * 64 + 128, :] = apply(0, high, low)

    def group(g, carry):
        base = g * 8
        at = pl.ds(pl.multiple_of(base, 8), 8)
        spec = [(y_ref[at, :128], None)]
        for k in range(1, 16):
            at = pl.ds(pl.multiple_of(base + k * ROWS, 8), 8)
            re, im = y_ref[at, :128], y_ref[at, 128:]
            c, s = tc_ref[k : k + 1, :], ts_ref[k : k + 1, :]
            spec.append((re * c - im * s, im * c + re * s))
        at = pl.ds(pl.multiple_of(base, 8), 8)
        spec.append((y_ref[at, 128:], None))
        for a, value in enumerate(real_inverse(spec)):
            out_ref[at, a * TILE : (a + 1) * TILE] = value
        return carry

    lax.fori_loop(0, 8, group, 0)
    for a in range(32):
        cols = slice(a * TILE, (a + 1) * TILE)
        support = hits_ref[a]
        updated = vol_ref[:, cols].astype(F32) * support + out_ref[:, cols]
        out_ref[:, cols] = support * (updated - jnp.clip(updated, -THRESHOLD, THRESHOLD))


def call(kernel, out_shape, operands, places, scratch):
    spaces = {"s": pltpu.SMEM, "v": pltpu.VMEM, "h": pltpu.HBM}
    operands = [
        pltpu.with_memory_space_constraint(x, pltpu.HBM) if place == "h" else x for x, place in zip(operands, places)
    ]
    return pl.pallas_call(
        kernel,
        out_shape=jax.ShapeDtypeStruct(out_shape, F32),
        in_specs=[pl.BlockSpec(memory_space=spaces[place]) for place in places],
        out_specs=pl.BlockSpec(memory_space=pltpu.VMEM),
        scratch_shapes=scratch,
        compiler_params=pltpu.CompilerParams(vmem_limit_bytes=VMEM_LIMIT),
    )(*operands)


def rows_step(tiles, depth, volume, hologram):
    wt = np.concatenate([matrix_forward().T, matrix_first_slot().T], axis=0)
    return call(
        rows_kernel,
        (2560, 128),
        (depth, tiles, volume, hologram, np.concatenate(twist_tables()), split_np(wt)),
        "shhhhh",
        [
            pltpu.SMEM((16, 32), jnp.int32),
            pltpu.VMEM((2 * ROWS, N), BF16),
            pltpu.VMEM((64, 128), F32),
            pltpu.VMEM((2, 512, 256), BF16),
            pltpu.VMEM((2048, 256), F32),
            pltpu.SMEM((80,), F32),
            pltpu.SemaphoreType.DMA((5,)),
        ],
    )


def columns_step(received):
    tc, ts = twist_tables()
    return call(
        columns_kernel,
        (2048, 128),
        (received, tc, ts, split_np(matrix_forward()), split_np(matrix_inverse())),
        "vvvvv",
        [
            pltpu.VMEM((1024, 128), F32),
            pltpu.VMEM((1920, 128), F32),
            pltpu.VMEM((1920, 128), F32),
            pltpu.VMEM((160, 128), F32),
        ],
    )


def update_step(tiles, volume, received):
    tc, ts = twist_tables()
    wi = split_np(np.stack([matrix_inverse(), matrix_first_slot_inverse()]))
    return call(
        update_kernel,
        (ROWS, N),
        (tiles, volume, received, tc, ts, wi),
        "svvvvv",
        [pltpu.VMEM((1024, 256), F32), pltpu.SMEM((40,), F32)],
    )


def exchange(value, shape):
    moved = lax.all_to_all(value.reshape(shape), ("lat", "depth"), split_axis=0, concat_axis=0, tiled=True)
    return moved.reshape(value.shape)


def body(volume, hologram, plane_depth, tile_list):
    tiles, volume = tile_list[0].T, volume[0]
    spectra = rows_step(tiles, plane_depth, volume, hologram)
    spectra = exchange(spectra, (512, 1, 640))
    filtered = columns_step(spectra)
    filtered = exchange(filtered, (512, 4, 128))
    return update_step(tiles, volume, filtered)[None]


def solution(mesh):
    return jax.shard_map(
        body,
        mesh=mesh,
        in_specs=(P("depth", "lat", None), P("lat", None), P("depth"), P("depth", None, None)),
        out_specs=P("depth", "lat", None),
        check_vma=False,
    )
```

```python
import functools
import math

import jax
import jax.numpy as jnp
import ml_dtypes
import numpy as np
from jax import lax
from jax.experimental import pallas as pl
from jax.experimental.pallas import tpu as pltpu
from jax.sharding import PartitionSpec as P


TILE = 128
N = 4096
ROWS = 64
PLANES = 8
TWO_PI = 2.0 * math.pi
WAVE_RATIO = 0.266
DEPTH_SCALE = 0.001 / 5.32e-07
STEP_SIZE = 0.1
THRESHOLD = 0.25
F32 = jnp.float32
BF16 = jnp.bfloat16
VMEM_LIMIT = 48 * 1024 * 1024
PRODUCT_ROWS = 512


def split_np(table):
    table = np.asarray(table, np.float64)
    high = table.astype(ml_dtypes.bfloat16)
    low = (table - high.astype(np.float64)).astype(ml_dtypes.bfloat16)
    return np.stack([high, low])


def twist_tables():
    k = np.arange(32)[:, None]
    b = np.arange(128)[None, :]
    angle = TWO_PI * ((k * b) % N) / N
    return np.cos(angle).astype(np.float32), np.sin(angle).astype(np.float32)


def matrix_forward():
    b = np.arange(128)
    angle = TWO_PI * ((b[:, None] * b[None, :]) % 128) / 128
    cos, sin = np.cos(angle), np.sin(angle)
    return np.block([[cos, -sin], [sin, cos]])


def matrix_inverse():
    return matrix_forward().T


def matrix_first_slot():
    b = np.arange(128)[:, None]
    m = np.arange(64)[None, :]
    low = TWO_PI * ((b * 32 * m) % N) / N
    high = TWO_PI * ((b * (16 + 32 * m)) % N) / N
    out = np.zeros((256, 256))
    out[:128, :64] = np.cos(low)
    out[:128, 128:192] = -np.sin(low)
    out[:128, 128] = 1.0 - 2.0 * (np.arange(128) % 2)
    out[128:, 64:128] = np.cos(high)
    out[128:, 192:] = -np.sin(high)
    return out


def matrix_first_slot_inverse():
    out = 2.0 * matrix_first_slot().T
    out[0] *= 0.5
    out[128] *= 0.5
    return out


def cosine_coefficients():
    nodes = 0.125 * (1.0 - np.cos(np.pi * (np.arange(64) + 0.5) / 64))
    values = np.cos(TWO_PI * np.sqrt(nodes))
    fit = np.polynomial.chebyshev.Chebyshev.fit(nodes, values, 6, domain=[0.0, 0.25])
    return [float(v) for v in fit.convert(kind=np.polynomial.Polynomial).coef]


COSINE = cosine_coefficients()


def turned(re, im, index, length, sign):
    index = index % length
    if index == 0:
        return re, im
    if 4 * index == length:
        if im is None:
            return None, (re if sign > 0 else -re)
        return (-im, re) if sign > 0 else (im, -re)
    c = math.cos(TWO_PI * index / length)
    s = sign * math.sin(TWO_PI * index / length)
    if im is None:
        return re * c, re * s
    if 8 * index == length:
        return ((re - im) * c, (re + im) * c) if sign > 0 else ((re + im) * c, (im - re) * c)
    if 8 * index == 3 * length:
        c = -c
        return (-((re + im) * c), (re - im) * c) if sign > 0 else ((im - re) * c, -((re + im) * c))
    return re * c - im * s, re * s + im * c


def plus(a, b):
    return b if a is None else (a if b is None else a + b)


def minus(a, b):
    if b is None:
        return a
    return -b if a is None else a - b


def real_forward(values):
    length = len(values)
    if length == 2:
        return [(values[0] + values[1], None), (values[0] - values[1], None)]
    even = real_forward(values[0::2])
    odd = real_forward(values[1::2])
    out = [None] * (length // 2 + 1)
    for k in range(length // 4 + 1):
        er, ei = even[k]
        tr, ti = turned(odd[k][0], odd[k][1], k, length, -1)
        out[k] = (plus(er, tr), plus(ei, ti))
        if 4 * k != length:
            out[length // 2 - k] = (minus(er, tr), minus(ti, ei))
    return out


def real_inverse(spectrum):
    length = 2 * (len(spectrum) - 1)
    if length == 2:
        return [spectrum[0][0] + spectrum[1][0], spectrum[0][0] - spectrum[1][0]]
    even, odd = [], []
    for k in range(length // 4 + 1):
        zr, zi = spectrum[k]
        yr, yi = spectrum[length // 2 - k]
        if 4 * k == length:
            even.append((zr + zr, None))
            odd.append((-(zi + zi), None))
            continue
        even.append((zr + yr, minus(zi, yi)))
        odd.append(turned(zr - yr, plus(zi, yi), k, length, 1))
    out = [None] * length
    out[0::2] = real_inverse(even)
    out[1::2] = real_inverse(odd)
    return out


def complex_sum(values, sign):
    length = len(values)
    if length == 1:
        return values
    even = complex_sum(values[0::2], sign)
    odd = complex_sum(values[1::2], sign)
    out = [None] * length
    for k in range(length // 2):
        er, ei = even[k]
        tr, ti = turned(odd[k][0], odd[k][1], k, length, sign)
        out[k] = (er + tr, ei + ti)
        out[k + length // 2] = (er - tr, ei - ti)
    return out


def parts(value):
    high = value.astype(BF16)
    return high, (value - high.astype(F32)).astype(BF16)


def mm(a, b, transposed=False):
    dims = (((1,), (1,)), ((), ())) if transposed else (((1,), (0,)), ((), ()))
    return lax.dot_general(a, b, dims, preferred_element_type=F32)


def lanes_of(shape):
    return lax.broadcasted_iota(jnp.int32, shape, len(shape) - 1)


def places():
    return lax.axis_index("depth"), lax.axis_index("lat")


def mark_tiles(tiles_ref, hits_ref, lat_place):
    for t in range(40):
        hits_ref[t] = 0.0
    for slot in range(16):
        hits_ref[tiles_ref[slot, lat_place // 2]] = 1.0


def rows_kernel(
    depth_ref, tiles_hbm, vol_hbm, holo_hbm, tw_hbm, wt_hbm, out_ref, mask_ref, tiles_ref, src_ref, tw, wt_ref, y_ref, hits_ref, sems
):
    copies = [
        pltpu.make_async_copy(tiles_hbm, tiles_ref, sems.at[0]),
        pltpu.make_async_copy(vol_hbm, src_ref.at[0:ROWS], sems.at[1]),
        pltpu.make_async_copy(tw_hbm, tw, sems.at[2]),
        pltpu.make_async_copy(holo_hbm, src_ref.at[ROWS : 2 * ROWS], sems.at[3]),
        pltpu.make_async_copy(wt_hbm, wt_ref, sems.at[4]),
    ]
    for copy in copies:
        copy.start()
    depth_place, lat_place = places()
    copies[0].wait()
    mark_tiles(tiles_ref, hits_ref, lat_place)
    for a in range(32):
        mask_ref[a : a + 1, :] = jnp.full((1, 128), hits_ref[a], F32)

    def group(masked, g, carry):
        rows = pl.ds(pl.multiple_of(g * 16 + (0 if masked else ROWS), 16), 16)
        values = []
        for a in range(32):
            tile = src_ref[rows, a * TILE : (a + 1) * TILE].astype(F32)
            values.append(tile * mask_ref[a : a + 1, :] if masked else tile)
        base = g * 16 + (0 if masked else 1024)
        spec = real_forward(values)
        at = pl.ds(pl.multiple_of(base, 16), 16)
        y_ref[at, :128] = spec[0][0]
        y_ref[at, 128:] = spec[16][0]
        for k in range(1, 16):
            at = pl.ds(pl.multiple_of(base + k * ROWS, 16), 16)
            re, im = spec[k]
            c, s = tw[k : k + 1, :], tw[32 + k : 33 + k, :]
            y_ref[at, :128] = re * c + im * s
            y_ref[at, 128:] = im * c - re * s
        return carry

    copies[1].wait()
    copies[2].wait()
    lax.fori_loop(0, 4, functools.partial(group, True), 0)
    copies[3].wait()
    lax.fori_loop(0, 4, functools.partial(group, False), 0)
    copies[4].wait()

    def apply(start, size, high, low):
        w_high, w_low = wt_ref[0, pl.ds(start, size), :], wt_ref[1, pl.ds(start, size), :]
        return mm(w_high, high, True) + (mm(w_high, low, True) + mm(w_low, high, True))

    for sg in range(4):
        high, low = parts(y_ref[sg * 256 : (sg + 1) * 256, :])
        o = apply(0, 256, high, low)
        for h in range(2):
            part = o[:, h * 128 : (h + 1) * 128]
            if sg == 0 and h == 0:
                first = apply(256, 256, high[:128], low[:128])
                part = jnp.where(lanes_of(part.shape) < ROWS, first, part)
            for c in range(2):
                out_ref[pl.ds(sg * 640 + c * 2 + h, 128, stride=5), :] = part[c * 128 : (c + 1) * 128]

    depth = depth_ref[0]
    half, slot_low = depth_place // 4, depth_place % 4
    for sg in range(4):
        slot = sg * 4 + slot_low
        y = y_ref[pl.ds(pl.multiple_of(1024 + slot * ROWS, ROWS), ROWS), :]
        high, low = parts(jnp.concatenate([y, y], axis=0))
        start = half * 128
        if sg == 0:
            start = start + jnp.where(slot_low == 0, 256, 0)
        o = apply(pl.multiple_of(start, 128), 128, high, low)
        out_ref[pl.ds(sg * 640 + 4, 128, stride=5), :] = jnp.where(lanes_of(o.shape) < ROWS, o, depth)


def signed(index):
    return jnp.where(index < N // 2, index, index - N)


def cosine(turns):
    rest = turns - jnp.round(turns)
    square = rest * rest
    value = COSINE[-1] * square + COSINE[-2]
    for coefficient in COSINE[-3::-1]:
        value = value * square + coefficient
    return value


def columns_kernel(in_ref, tc_ref, ts_ref, w_ref, wi_ref, out_ref, x_ref, zr_ref, zi_ref, bend_ref):
    depth_place, lat_place = places()
    place = lat_place * PLANES + depth_place
    first = place == 0
    slot_group, col = place // 128, place % 128
    left = lanes_of((8, 128)) < ROWS
    fourth = lax.broadcasted_iota(jnp.int32, (8, 128), 0) % 4 == 0
    zero = jnp.zeros((8, 128), F32)

    def swap(value):
        return pltpu.roll(value, ROWS, 1)

    def exchanged(p, q):
        middle = swap(jnp.where(left, q, p))
        return jnp.where(left, p, middle), jnp.where(left, middle, q)

    def x_at(g, a, c):
        return pl.ds(pl.multiple_of(g * 512 + a * 16 + c * 8, 8), 8)

    def received(a, upper, q):
        return in_ref[pl.ds(a * 80 + upper * 40 + q, 8, stride=5), :]

    def store_spectrum(g, k, re, im):
        if k > 0:
            c, s = tc_ref[k : k + 1, :], ts_ref[k : k + 1, :]
            re, im = re * c + im * s, im * c - re * s
        at = pl.ds(g * 320 + k, 8, stride=40)
        zr_ref[at, :] = re
        zi_ref[at, :] = im

    ky = lax.broadcasted_iota(jnp.int32, (32, 128), 0) + 32 * lax.broadcasted_iota(jnp.int32, (32, 128), 1)
    uy = signed(ky).astype(F32) * (WAVE_RATIO / N)
    for g in range(5):
        if g == 4:
            kx = jnp.full((32, 128), -(N // 2), jnp.int32)
        else:
            slot = slot_group * 4 + g
            kx = slot + 32 * col
            if g == 0:
                kx = jnp.where(slot == 0, jnp.where(col < 64, 32 * col, 16 + 32 * (col - 64)), kx)
            kx = signed(jnp.full((32, 128), kx, jnp.int32))
        ux = kx.astype(F32) * (WAVE_RATIO / N)
        squared = uy * uy + ux * ux
        bend_ref[g * 32 : (g + 1) * 32, :] = squared / (1.0 + jnp.sqrt(1.0 - squared))

    def forward(h, carry):
        packed = jnp.logical_and(jnp.logical_and(first, h == 0), left)
        halves = []
        for upper in range(2):
            values = []
            for a in range(32):
                re, im = received(a, upper, h), received(a, upper, 2 + h)
                values.append((re, jnp.where(packed, zero, im)))
            halves.append(complex_sum(values, -1))
        for k in range(32):
            lower, upper = halves[0][k], halves[1][k]
            for number, column in enumerate(zip(*[exchanged(p, q) for p, q in zip(lower, upper)])):
                store_spectrum(2 * h + number, k, *column)
        return carry

    lax.fori_loop(0, 2, forward, 0)

    def gather(a, carry):
        both = jnp.where(left, received(a, 0, 4), swap(received(a, 1, 4)))
        x_ref[x_at(0, a, 0), :] = both
        x_ref[x_at(0, a, 1), :] = jnp.where(jnp.logical_and(first, fourth), zero, pltpu.roll(both, 4, 0))
        both = jnp.where(left, received(a, 0, 2), swap(received(a, 1, 2)))
        x_ref[x_at(1, a, 0), :] = jnp.where(first, both, zero)
        x_ref[x_at(1, a, 1), :] = zero
        return carry

    lax.fori_loop(0, 32, gather, 0, unroll=8)

    def forward_extra(g, carry):
        values = [(x_ref[x_at(g, a, 0), :], x_ref[x_at(g, a, 1), :]) for a in range(32)]
        for k, (re, im) in enumerate(complex_sum(values, -1)):
            store_spectrum(4 + g, k, re, im)
        return carry

    lax.fori_loop(0, 2, forward_extra, 0)

    def product(start, size, table):
        slabs = [slice((r // 32) * 40, (r // 32) * 40 + 32) for r in range(start, start + size, 32)]
        pairs = [parts(jnp.concatenate([ref[at, :] for at in slabs], axis=0)) for ref in (zr_ref, zi_ref)]
        high = jnp.concatenate([pairs[0][0], pairs[1][0]], axis=1)
        low = jnp.concatenate([pairs[0][1], pairs[1][1]], axis=1)
        value = mm(high, table[0]) + (mm(low, table[0]) + mm(high, table[1]))
        for i, at in enumerate(slabs):
            zr_ref[at, :] = value[i * 32 : (i + 1) * 32, :128]
            zi_ref[at, :] = value[i * 32 : (i + 1) * 32, 128:]

    for start in range(0, 1536, PRODUCT_ROWS):
        product(start, PRODUCT_ROWS, w_ref)

    scales = []
    for p in range(PLANES):
        row = jnp.broadcast_to(in_ref[p * 5 + 4 : p * 5 + 5, :], (8, 128))
        scales.append(DEPTH_SCALE * jnp.where(left, swap(row), row))
    gain = STEP_SIZE * 2.0 / (N * N)

    def mix(j, carry):
        extra = None
        for index, g in ((4, 5), (0, 0), (1, 1), (2, 2), (3, 3)):
            bend = bend_ref[pl.ds(pl.multiple_of(index * 32 + j * 8, 8), 8), :]
            waves = [cosine(scale * bend) for scale in scales]
            rows = [pl.ds(pl.multiple_of(g * 320 + p * 40 + j * 8, 8), 8) for p in range(PLANES)]
            at = pl.ds(pl.multiple_of(1280 + index * 40 + j * 8, 8), 8)
            scaled = []
            for ref in (zr_ref, zi_ref):
                terms = [wave * ref[row, :] for wave, row in zip(waves, rows)]
                while len(terms) > 1:
                    terms = [p + q for p, q in zip(terms[0::2], terms[1::2])]
                scaled.append((ref[at, :] - 2.0 * terms[0]) * gain)
            if index == 4:
                extra = [jnp.where(first, value, zero) for value in scaled], waves
                continue
            for p, row in enumerate(rows):
                re, im = waves[p] * scaled[0], waves[p] * scaled[1]
                if index == 0:
                    re = re - extra[1][p] * extra[0][1]
                    im = im + extra[1][p] * extra[0][0]
                zr_ref[row, :] = re
                zi_ref[row, :] = im
        return carry

    lax.fori_loop(0, 4, mix, 0)

    for start in range(0, 1024, PRODUCT_ROWS):
        product(start, PRODUCT_ROWS, wi_ref)

    def backward(h, carry):
        lower, upper = [], []
        for k in range(32):
            columns = []
            for g in (2 * h, 2 * h + 1):
                at = pl.ds(g * 320 + k, 8, stride=40)
                re, im = zr_ref[at, :], zi_ref[at, :]
                if k > 0:
                    c, s = tc_ref[k : k + 1, :], ts_ref[k : k + 1, :]
                    re, im = re * c - im * s, im * c + re * s
                columns.append((re, im))
            halves = list(zip(*[exchanged(p, q) for p, q in zip(*columns)]))
            lower.append(halves[0])
            upper.append(halves[1])
        for number, values in enumerate((lower, upper)):
            for a, (re, im) in enumerate(complex_sum(values, 1)):
                out_ref[pl.ds(a * 64 + number * 32 + h, 8, stride=4), :] = re
                out_ref[pl.ds(a * 64 + number * 32 + 2 + h, 8, stride=4), :] = im
        return carry

    lax.fori_loop(0, 2, backward, 0)


def update_kernel(mask_ref, vol_ref, in_ref, tc_ref, ts_ref, wi_ref, out_hbm, y_ref, new_ref, sems):
    def apply(which, high, low):
        w_high, w_low = wi_ref[0, which], wi_ref[1, which]
        return mm(high, w_high) + (mm(low, w_high) + mm(high, w_low))

    for sg in range(4):
        for h in range(2):
            blocks = [in_ref[pl.ds(sg * 512 + c * 2 + h, 128, stride=4), :].T for c in range(2)]
            high, low = parts(jnp.concatenate(blocks, axis=1))
            slot = sg * 4 + h * 2
            if slot == 0:
                y_ref[0:64, :] = apply(1, high[:64], low[:64])
                y_ref[64:128, :] = apply(0, high[64:], low[64:])
            else:
                y_ref[slot * 64 : slot * 64 + 128, :] = apply(0, high, low)

    def copy_out(g):
        rows = pl.ds(pl.multiple_of(g * 16, 16), 16)
        return pltpu.make_async_copy(new_ref.at[rows], out_hbm.at[rows], sems.at[g])

    def group(g, carry):
        rows = pl.ds(pl.multiple_of(g * 16, 16), 16)
        spec = [(y_ref[rows, :128], None)]
        for k in range(1, 16):
            at = pl.ds(pl.multiple_of(g * 16 + k * ROWS, 16), 16)
            re, im = y_ref[at, :128], y_ref[at, 128:]
            c, s = tc_ref[k : k + 1, :], ts_ref[k : k + 1, :]
            spec.append((re * c - im * s, im * c + re * s))
        spec.append((y_ref[rows, 128:], None))
        for a, step in enumerate(real_inverse(spec)):
            cols = slice(a * TILE, (a + 1) * TILE)
            support = mask_ref[a : a + 1, :]
            updated = vol_ref[rows, cols].astype(F32) * support + step
            new_ref[rows, cols] = support * (updated - jnp.clip(updated, -THRESHOLD, THRESHOLD))
        copy_out(g).start()
        return carry

    lax.fori_loop(0, 4, group, 0)
    for g in range(4):
        copy_out(g).wait()


def call(kernel, out_shapes, operands, places, scratch):
    spaces = {"s": pltpu.SMEM, "v": pltpu.VMEM, "h": pltpu.HBM}
    specs = [pl.BlockSpec(memory_space=spaces[place]) for place in places]
    operands = [
        pltpu.with_memory_space_constraint(x, pltpu.HBM) if place == "h" else x for x, place in zip(operands, places)
    ]
    return pl.pallas_call(
        kernel,
        out_shape=[jax.ShapeDtypeStruct(shape, F32) for shape in out_shapes],
        in_specs=specs[: len(operands)],
        out_specs=specs[len(operands) :],
        scratch_shapes=scratch,
        compiler_params=pltpu.CompilerParams(vmem_limit_bytes=VMEM_LIMIT),
    )(*operands)


def rows_step(tiles, depth, volume, hologram):
    wt = np.concatenate([matrix_forward().T, matrix_first_slot().T], axis=0)
    return call(
        rows_kernel,
        [(2560, 128), (32, 128)],
        (depth, tiles, volume, hologram, np.concatenate(twist_tables()), split_np(wt)),
        "shhhhhvv",
        [
            pltpu.SMEM((16, 32), jnp.int32),
            pltpu.VMEM((2 * ROWS, N), BF16),
            pltpu.VMEM((64, 128), F32),
            pltpu.VMEM((2, 512, 256), BF16),
            pltpu.VMEM((2048, 256), F32),
            pltpu.SMEM((40,), F32),
            pltpu.SemaphoreType.DMA((5,)),
        ],
    )


def columns_step(received):
    tc, ts = twist_tables()
    return call(
        columns_kernel,
        [(2048, 128)],
        (received, tc, ts, split_np(matrix_forward()), split_np(matrix_inverse())),
        "vvvvvv",
        [
            pltpu.VMEM((1024, 128), F32),
            pltpu.VMEM((1920, 128), F32),
            pltpu.VMEM((1920, 128), F32),
            pltpu.VMEM((160, 128), F32),
        ],
    )


def update_step(mask, volume, received):
    tc, ts = twist_tables()
    wi = split_np(np.stack([matrix_inverse(), matrix_first_slot_inverse()]))
    return call(
        update_kernel,
        [(ROWS, N)],
        (mask, volume, received, tc, ts, wi),
        "vvvvvvh",
        [pltpu.VMEM((1024, 256), F32), pltpu.VMEM((ROWS, N), F32), pltpu.SemaphoreType.DMA((4,))],
    )


def exchange(value, shape):
    moved = lax.all_to_all(value.reshape(shape), ("lat", "depth"), split_axis=0, concat_axis=0, tiled=True)
    return moved.reshape(value.shape)


def body(volume, hologram, plane_depth, tile_list):
    tiles, volume = tile_list[0].T, volume[0]
    spectra, mask = rows_step(tiles, plane_depth, volume, hologram)
    spectra = exchange(spectra, (512, 1, 640))
    (filtered,) = columns_step(spectra)
    filtered = exchange(filtered, (512, 4, 128))
    (updated,) = update_step(mask, volume, filtered)
    return updated[None]


def solution(mesh):
    return jax.shard_map(
        body,
        mesh=mesh,
        in_specs=(P("depth", "lat", None), P("lat", None), P("depth"), P("depth", None, None)),
        out_specs=P("depth", "lat", None),
        check_vma=False,
    )
```

```python
import math

import jax
import jax.numpy as jnp
import ml_dtypes
import numpy as np
from jax import lax
from jax.experimental import pallas as pl
from jax.experimental.pallas import tpu as pltpu
from jax.sharding import PartitionSpec as P


TILE = 128
N = 4096
ROWS = 64
PLANES = 8
TWO_PI = 2.0 * math.pi
WAVE_RATIO = 0.266
DEPTH_SCALE = 0.001 / 5.32e-07
STEP_SIZE = 0.1
THRESHOLD = 0.25
F32 = jnp.float32
BF16 = jnp.bfloat16
VMEM_LIMIT = 48 * 1024 * 1024


def split_np(table):
    table = np.asarray(table, np.float64)
    high = table.astype(ml_dtypes.bfloat16)
    low = (table - high.astype(np.float64)).astype(ml_dtypes.bfloat16)
    return np.stack([high, low])


def twist_tables():
    k = np.arange(32)[:, None]
    b = np.arange(128)[None, :]
    angle = TWO_PI * ((k * b) % N) / N
    return np.cos(angle).astype(np.float32), np.sin(angle).astype(np.float32)


def matrix_forward():
    b = np.arange(128)
    angle = TWO_PI * ((b[:, None] * b[None, :]) % 128) / 128
    cos, sin = np.cos(angle), np.sin(angle)
    return np.block([[cos, -sin], [sin, cos]])


def matrix_inverse():
    return matrix_forward().T


def matrix_first_slot():
    b = np.arange(128)[:, None]
    m = np.arange(64)[None, :]
    low = TWO_PI * ((b * 32 * m) % N) / N
    high = TWO_PI * ((b * (16 + 32 * m)) % N) / N
    out = np.zeros((256, 256))
    out[:128, :64] = np.cos(low)
    out[:128, 128:192] = -np.sin(low)
    out[:128, 128] = 1.0 - 2.0 * (np.arange(128) % 2)
    out[128:, 64:128] = np.cos(high)
    out[128:, 192:] = -np.sin(high)
    return out


def matrix_first_slot_inverse():
    out = 2.0 * matrix_first_slot().T
    out[0] *= 0.5
    out[128] *= 0.5
    return out


def cosine_coefficients():
    nodes = 0.125 * (1.0 - np.cos(np.pi * (np.arange(64) + 0.5) / 64))
    values = np.cos(TWO_PI * np.sqrt(nodes))
    fit = np.polynomial.chebyshev.Chebyshev.fit(nodes, values, 6, domain=[0.0, 0.25])
    return [float(v) for v in fit.convert(kind=np.polynomial.Polynomial).coef]


COSINE = cosine_coefficients()


def turned(re, im, index, length, sign):
    index = index % length
    if index == 0:
        return re, im
    if 4 * index == length:
        if im is None:
            return None, (re if sign > 0 else -re)
        return (-im, re) if sign > 0 else (im, -re)
    c = math.cos(TWO_PI * index / length)
    s = sign * math.sin(TWO_PI * index / length)
    if im is None:
        return re * c, re * s
    if 8 * index == length:
        return ((re - im) * c, (re + im) * c) if sign > 0 else ((re + im) * c, (im - re) * c)
    if 8 * index == 3 * length:
        c = -c
        return (-((re + im) * c), (re - im) * c) if sign > 0 else ((im - re) * c, -((re + im) * c))
    return re * c - im * s, re * s + im * c


def plus(a, b):
    return b if a is None else (a if b is None else a + b)


def minus(a, b):
    if b is None:
        return a
    return -b if a is None else a - b


def real_forward(values):
    length = len(values)
    if length == 2:
        return [(values[0] + values[1], None), (values[0] - values[1], None)]
    even = real_forward(values[0::2])
    odd = real_forward(values[1::2])
    out = [None] * (length // 2 + 1)
    for k in range(length // 4 + 1):
        er, ei = even[k]
        tr, ti = turned(odd[k][0], odd[k][1], k, length, -1)
        out[k] = (plus(er, tr), plus(ei, ti))
        if 4 * k != length:
            out[length // 2 - k] = (minus(er, tr), minus(ti, ei))
    return out


def real_inverse(spectrum):
    length = 2 * (len(spectrum) - 1)
    if length == 2:
        return [spectrum[0][0] + spectrum[1][0], spectrum[0][0] - spectrum[1][0]]
    even, odd = [], []
    for k in range(length // 4 + 1):
        zr, zi = spectrum[k]
        yr, yi = spectrum[length // 2 - k]
        if 4 * k == length:
            even.append((zr + zr, None))
            odd.append((-(zi + zi), None))
            continue
        even.append((zr + yr, minus(zi, yi)))
        odd.append(turned(zr - yr, plus(zi, yi), k, length, 1))
    out = [None] * length
    out[0::2] = real_inverse(even)
    out[1::2] = real_inverse(odd)
    return out


def complex_sum(values, sign):
    length = len(values)
    if length == 1:
        return values
    even = complex_sum(values[0::2], sign)
    odd = complex_sum(values[1::2], sign)
    out = [None] * length
    for k in range(length // 2):
        er, ei = even[k]
        tr, ti = turned(odd[k][0], odd[k][1], k, length, sign)
        out[k] = (er + tr, ei + ti)
        out[k + length // 2] = (er - tr, ei - ti)
    return out


def parts(value):
    high = value.astype(BF16)
    return high, (value - high.astype(F32)).astype(BF16)


def mm(a, b, transposed=False):
    dims = (((1,), (1,)), ((), ())) if transposed else (((1,), (0,)), ((), ()))
    return lax.dot_general(a, b, dims, preferred_element_type=F32)


def lanes_of(shape):
    return lax.broadcasted_iota(jnp.int32, shape, len(shape) - 1)


def places():
    return lax.axis_index("depth"), lax.axis_index("lat")


def mark_tiles(tiles_ref, hits_ref, lat_place):
    for t in range(40):
        hits_ref[t] = 0.0
    for slot in range(16):
        hits_ref[tiles_ref[slot, lat_place // 2]] = 1.0


def rows_kernel(
    depth_ref, tiles_hbm, vol_hbm, holo_hbm, tw_hbm, wt_hbm, out_ref, mask_ref, tiles_ref, src_ref, tw, wt_ref, y_ref, hits_ref, sems
):
    copies = [
        pltpu.make_async_copy(tiles_hbm, tiles_ref, sems.at[0]),
        pltpu.make_async_copy(vol_hbm, src_ref.at[0:ROWS], sems.at[1]),
        pltpu.make_async_copy(tw_hbm, tw, sems.at[2]),
        pltpu.make_async_copy(holo_hbm, src_ref.at[ROWS : 2 * ROWS], sems.at[3]),
        pltpu.make_async_copy(wt_hbm, wt_ref, sems.at[4]),
    ]
    for copy in copies:
        copy.start()
    depth_place, lat_place = places()
    copies[0].wait()
    mark_tiles(tiles_ref, hits_ref, lat_place)
    for a in range(32):
        mask_ref[a : a + 1, :] = jnp.full((1, 128), hits_ref[a], F32)

    def group(masked, g):
        start = g * 16 + (0 if masked else ROWS)
        rows = slice(start, start + 16)
        values = []
        for a in range(32):
            tile = src_ref[rows, a * TILE : (a + 1) * TILE].astype(F32)
            values.append(tile * mask_ref[a : a + 1, :] if masked else tile)
        base = g * 16 + (0 if masked else 1024)
        spec = real_forward(values)
        at = slice(base, base + 16)
        y_ref[at, :128] = spec[0][0]
        y_ref[at, 128:] = spec[16][0]
        for k in range(1, 16):
            at = slice(base + k * ROWS, base + k * ROWS + 16)
            re, im = spec[k]
            c, s = tw[k : k + 1, :], tw[32 + k : 33 + k, :]
            y_ref[at, :128] = re * c + im * s
            y_ref[at, 128:] = im * c - re * s

    copies[1].wait()
    copies[2].wait()
    for g in range(4):
        group(True, g)
    copies[3].wait()
    copies[4].wait()

    def apply(start, size, high, low):
        w_high, w_low = wt_ref[0, pl.ds(start, size), :], wt_ref[1, pl.ds(start, size), :]
        return mm(w_high, high, True) + (mm(w_high, low, True) + mm(w_low, high, True))

    for g in range(4):
        group(False, g)
    for sg in range(4):
        high, low = parts(y_ref[sg * 256 : (sg + 1) * 256, :])
        o = apply(0, 256, high, low)
        for h in range(2):
            part = o[:, h * 128 : (h + 1) * 128]
            if sg == 0 and h == 0:
                first = apply(256, 256, high[:128], low[:128])
                part = jnp.where(lanes_of(part.shape) < ROWS, first, part)
            for c in range(2):
                out_ref[pl.ds(sg * 640 + c * 2 + h, 128, stride=5), :] = part[c * 128 : (c + 1) * 128]

    depth = depth_ref[0]
    half, slot_low = depth_place // 4, depth_place % 4
    for sg in range(4):
        slot = sg * 4 + slot_low
        y = y_ref[pl.ds(pl.multiple_of(1024 + slot * ROWS, ROWS), ROWS), :]
        high, low = parts(jnp.concatenate([y, y], axis=0))
        start = half * 128
        if sg == 0:
            start = start + jnp.where(slot_low == 0, 256, 0)
        o = apply(pl.multiple_of(start, 128), 128, high, low)
        out_ref[pl.ds(sg * 640 + 4, 128, stride=5), :] = jnp.where(lanes_of(o.shape) < ROWS, o, depth)


def signed(index):
    return jnp.where(index < N // 2, index, index - N)


def cosine(turns):
    rest = turns - jnp.round(turns)
    square = rest * rest
    value = COSINE[-1] * square + COSINE[-2]
    for coefficient in COSINE[-3::-1]:
        value = value * square + coefficient
    return value


def columns_kernel(in_ref, tc_ref, ts_ref, w_ref, wi_ref, out_ref, x_ref, zr_ref, zi_ref, bend_ref):
    depth_place, lat_place = places()
    place = lat_place * PLANES + depth_place
    first = place == 0
    slot_group, col = place // 128, place % 128
    left = lanes_of((8, 128)) < ROWS
    fourth = lax.broadcasted_iota(jnp.int32, (8, 128), 0) % 4 == 0
    zero = jnp.zeros((8, 128), F32)

    def swap(value):
        return pltpu.roll(value, ROWS, 1)

    def exchanged(p, q):
        middle = swap(jnp.where(left, q, p))
        return jnp.where(left, p, middle), jnp.where(left, middle, q)

    def x_at(g, a, c):
        return slice(g * 512 + a * 16 + c * 8, g * 512 + a * 16 + c * 8 + 8)

    def received(a, upper, q):
        return in_ref[pl.ds(a * 80 + upper * 40 + q, 8, stride=5), :]

    def store_spectrum(g, k, re, im):
        if k > 0:
            c, s = tc_ref[k : k + 1, :], ts_ref[k : k + 1, :]
            re, im = re * c + im * s, im * c - re * s
        at = pl.ds(g * 320 + k, 8, stride=40)
        zr_ref[at, :] = re
        zi_ref[at, :] = im

    ky = lax.broadcasted_iota(jnp.int32, (32, 128), 0) + 32 * lax.broadcasted_iota(jnp.int32, (32, 128), 1)
    uy = signed(ky).astype(F32) * (WAVE_RATIO / N)
    for g in range(5):
        if g == 4:
            kx = jnp.full((32, 128), -(N // 2), jnp.int32)
        else:
            slot = slot_group * 4 + g
            kx = slot + 32 * col
            if g == 0:
                kx = jnp.where(slot == 0, jnp.where(col < 64, 32 * col, 16 + 32 * (col - 64)), kx)
            kx = signed(jnp.full((32, 128), kx, jnp.int32))
        ux = kx.astype(F32) * (WAVE_RATIO / N)
        squared = uy * uy + ux * ux
        bend_ref[g * 32 : (g + 1) * 32, :] = squared / (1.0 + jnp.sqrt(1.0 - squared))

    def forward(h):
        packed = jnp.logical_and(first, left)
        halves = []
        for upper in range(2):
            values = []
            for a in range(32):
                re, im = received(a, upper, h), received(a, upper, 2 + h)
                values.append((re, jnp.where(packed, zero, im) if h == 0 else im))
            halves.append(complex_sum(values, -1))
        for k in range(32):
            lower, upper = halves[0][k], halves[1][k]
            for number, column in enumerate(zip(*[exchanged(p, q) for p, q in zip(lower, upper)])):
                store_spectrum(2 * h + number, k, *column)


    for a in range(32):
        both = jnp.where(left, received(a, 0, 4), swap(received(a, 1, 4)))
        x_ref[x_at(0, a, 0), :] = both
        x_ref[x_at(0, a, 1), :] = jnp.where(jnp.logical_and(first, fourth), zero, pltpu.roll(both, 4, 0))
        both = jnp.where(left, received(a, 0, 2), swap(received(a, 1, 2)))
        x_ref[x_at(1, a, 0), :] = jnp.where(first, both, zero)
        x_ref[x_at(1, a, 1), :] = zero

    for g in range(2):
        values = [(x_ref[x_at(g, a, 0), :], x_ref[x_at(g, a, 1), :]) for a in range(32)]
        for k, (re, im) in enumerate(complex_sum(values, -1)):
            store_spectrum(4 + g, k, re, im)

    def product(start, size, table):
        slabs = [slice((r // 32) * 40, (r // 32) * 40 + 32) for r in range(start, start + size, 32)]
        pairs = [parts(jnp.concatenate([ref[at, :] for at in slabs], axis=0)) for ref in (zr_ref, zi_ref)]
        high = jnp.concatenate([pairs[0][0], pairs[1][0]], axis=1)
        low = jnp.concatenate([pairs[0][1], pairs[1][1]], axis=1)
        value = mm(high, table[0]) + (mm(low, table[0]) + mm(high, table[1]))
        for i, at in enumerate(slabs):
            zr_ref[at, :] = value[i * 32 : (i + 1) * 32, :128]
            zi_ref[at, :] = value[i * 32 : (i + 1) * 32, 128:]

    forward(0)
    product(1024, 512, w_ref)
    forward(1)
    product(0, 512, w_ref)
    product(512, 512, w_ref)

    scales = []
    for p in range(PLANES):
        row = jnp.broadcast_to(in_ref[p * 5 + 4 : p * 5 + 5, :], (8, 128))
        scales.append(DEPTH_SCALE * jnp.where(left, swap(row), row))
    gain = STEP_SIZE * 2.0 / (N * N)

    def mix(index):
        g = 5 if index == 4 else index
        for j in range(4):
            bend = bend_ref[index * 32 + j * 8 : index * 32 + j * 8 + 8, :]
            waves = [cosine(scale * bend) for scale in scales]
            rows = [slice(g * 320 + p * 40 + j * 8, g * 320 + p * 40 + j * 8 + 8) for p in range(PLANES)]
            at = slice(1280 + index * 40 + j * 8, 1280 + index * 40 + j * 8 + 8)
            scaled = []
            for ref in (zr_ref, zi_ref):
                terms = [wave * ref[row, :] for wave, row in zip(waves, rows)]
                while len(terms) > 1:
                    terms = [p + q for p, q in zip(terms[0::2], terms[1::2])]
                scaled.append((ref[at, :] - 2.0 * terms[0]) * gain)
            if index == 4:
                scaled = [jnp.where(first, value, zero) for value in scaled]
            for p, row in enumerate(rows):
                re, im = waves[p] * scaled[0], waves[p] * scaled[1]
                if index == 0:
                    other = slice(row.start + 1600, row.stop + 1600)
                    re, im = re - zi_ref[other, :], im + zr_ref[other, :]
                zr_ref[row, :] = re
                zi_ref[row, :] = im

    mix(4)
    mix(0)
    product(0, 256, wi_ref)
    mix(1)
    product(256, 256, wi_ref)
    mix(2)
    product(512, 256, wi_ref)
    mix(3)
    product(768, 256, wi_ref)

    for h in range(2):
        lower, upper = [], []
        for k in range(32):
            columns = []
            for g in (2 * h, 2 * h + 1):
                at = pl.ds(g * 320 + k, 8, stride=40)
                re, im = zr_ref[at, :], zi_ref[at, :]
                if k > 0:
                    c, s = tc_ref[k : k + 1, :], ts_ref[k : k + 1, :]
                    re, im = re * c - im * s, im * c + re * s
                columns.append((re, im))
            halves = list(zip(*[exchanged(p, q) for p, q in zip(*columns)]))
            lower.append(halves[0])
            upper.append(halves[1])
        for number, values in enumerate((lower, upper)):
            for a, (re, im) in enumerate(complex_sum(values, 1)):
                out_ref[pl.ds(a * 64 + number * 32 + h, 8, stride=4), :] = re
                out_ref[pl.ds(a * 64 + number * 32 + 2 + h, 8, stride=4), :] = im


def update_kernel(mask_ref, vol_ref, in_ref, tc_ref, ts_ref, wi_ref, out_hbm, y_ref, high_ref, low_ref, new_ref, sems):
    def apply(which, high, low):
        w_high, w_low = wi_ref[0, which], wi_ref[1, which]
        return mm(high, w_high) + (mm(low, w_high) + mm(high, w_low))

    for sg in range(4):
        blocks = [[in_ref[pl.ds(sg * 512 + c * 2 + h, 128, stride=4), :].T for c in range(2)] for h in range(2)]
        high, low = parts(jnp.concatenate([jnp.concatenate(pair, axis=1) for pair in blocks], axis=0))
        high_ref[sg * 256 : (sg + 1) * 256, :] = high
        low_ref[sg * 256 : (sg + 1) * 256, :] = low
    y_ref[0:64, :] = apply(1, high_ref[0:64, :], low_ref[0:64, :])

    def copy_out(g):
        rows = slice(g * 16, g * 16 + 16)
        return pltpu.make_async_copy(new_ref.at[rows], out_hbm.at[rows], sems.at[g])

    for g in range(4):
        rows = slice(g * 16, g * 16 + 16)
        spots = [slice(g * 16 + k * ROWS, g * 16 + k * ROWS + 16) for k in range(1, 16)]
        value = apply(0, *[jnp.concatenate([ref[at, :] for at in spots], axis=0) for ref in (high_ref, low_ref)])
        spec = [(y_ref[rows, :128], None)]
        for k in range(1, 16):
            at = slice((k - 1) * 16, k * 16)
            re, im = value[at, :128], value[at, 128:]
            c, s = tc_ref[k : k + 1, :], ts_ref[k : k + 1, :]
            spec.append((re * c - im * s, im * c + re * s))
        spec.append((y_ref[rows, 128:], None))
        for a, step in enumerate(real_inverse(spec)):
            cols = slice(a * TILE, (a + 1) * TILE)
            support = mask_ref[a : a + 1, :]
            updated = vol_ref[rows, cols].astype(F32) * support + step
            new_ref[rows, cols] = support * (updated - jnp.clip(updated, -THRESHOLD, THRESHOLD))
        copy_out(g).start()
    for g in range(4):
        copy_out(g).wait()


def call(kernel, out_shapes, operands, places, scratch):
    spaces = {"s": pltpu.SMEM, "v": pltpu.VMEM, "h": pltpu.HBM}
    specs = [pl.BlockSpec(memory_space=spaces[place]) for place in places]
    operands = [
        pltpu.with_memory_space_constraint(x, pltpu.HBM) if place == "h" else x for x, place in zip(operands, places)
    ]
    return pl.pallas_call(
        kernel,
        out_shape=[jax.ShapeDtypeStruct(shape, F32) for shape in out_shapes],
        in_specs=specs[: len(operands)],
        out_specs=specs[len(operands) :],
        scratch_shapes=scratch,
        compiler_params=pltpu.CompilerParams(vmem_limit_bytes=VMEM_LIMIT),
    )(*operands)


def rows_step(tiles, depth, volume, hologram):
    wt = np.concatenate([matrix_forward().T, matrix_first_slot().T], axis=0)
    return call(
        rows_kernel,
        [(2560, 128), (32, 128)],
        (depth, tiles, volume, hologram, np.concatenate(twist_tables()), split_np(wt)),
        "shhhhhvv",
        [
            pltpu.SMEM((16, 32), jnp.int32),
            pltpu.VMEM((2 * ROWS, N), BF16),
            pltpu.VMEM((64, 128), F32),
            pltpu.VMEM((2, 512, 256), BF16),
            pltpu.VMEM((2048, 256), F32),
            pltpu.SMEM((40,), F32),
            pltpu.SemaphoreType.DMA((5,)),
        ],
    )


def columns_step(received):
    tc, ts = twist_tables()
    return call(
        columns_kernel,
        [(2048, 128)],
        (received, tc, ts, split_np(matrix_forward()), split_np(matrix_inverse())),
        "vvvvvv",
        [
            pltpu.VMEM((1024, 128), F32),
            pltpu.VMEM((1920, 128), F32),
            pltpu.VMEM((1920, 128), F32),
            pltpu.VMEM((160, 128), F32),
        ],
    )


def update_step(mask, volume, received):
    tc, ts = twist_tables()
    wi = split_np(np.stack([matrix_inverse(), matrix_first_slot_inverse()]))
    return call(
        update_kernel,
        [(ROWS, N)],
        (mask, volume, received, tc, ts, wi),
        "vvvvvvh",
        [pltpu.VMEM((64, 256), F32), pltpu.VMEM((1024, 256), BF16), pltpu.VMEM((1024, 256), BF16), pltpu.VMEM((ROWS, N), F32), pltpu.SemaphoreType.DMA((4,))],
    )


def exchange(value, shape):
    moved = lax.all_to_all(value.reshape(shape), ("lat", "depth"), split_axis=0, concat_axis=0, tiled=True)
    return moved.reshape(value.shape)


def body(volume, hologram, plane_depth, tile_list):
    tiles, volume = tile_list[0].T, volume[0]
    spectra, mask = rows_step(tiles, plane_depth, volume, hologram)
    spectra = exchange(spectra, (512, 1, 640))
    (filtered,) = columns_step(spectra)
    filtered = exchange(filtered, (512, 4, 128))
    (updated,) = update_step(mask, volume, filtered)
    return updated[None]


def solution(mesh):
    return jax.shard_map(
        body,
        mesh=mesh,
        in_specs=(P("depth", "lat", None), P("lat", None), P("depth"), P("depth", None, None)),
        out_specs=P("depth", "lat", None),
        check_vma=False,
    )
```

```python
import math

import jax
import jax.numpy as jnp
import ml_dtypes
import numpy as np
from jax import lax
from jax.experimental import pallas as pl
from jax.experimental.pallas import tpu as pltpu
from jax.sharding import PartitionSpec as P


TILE = 128
N = 4096
ROWS = 64
PLANES = 8
TWO_PI = 2.0 * math.pi
WAVE_RATIO = 0.266
DEPTH_SCALE = 0.001 / 5.32e-07
STEP_SIZE = 0.1
THRESHOLD = 0.25
F32 = jnp.float32
BF16 = jnp.bfloat16
VMEM_LIMIT = 48 * 1024 * 1024


def split_np(table):
    table = np.asarray(table, np.float64)
    high = table.astype(ml_dtypes.bfloat16)
    low = (table - high.astype(np.float64)).astype(ml_dtypes.bfloat16)
    return np.stack([high, low])


def twist_tables():
    k = np.arange(32)[:, None]
    b = np.arange(128)[None, :]
    angle = TWO_PI * ((k * b) % N) / N
    return np.cos(angle).astype(np.float32), np.sin(angle).astype(np.float32)


def matrix_forward():
    b = np.arange(128)
    angle = TWO_PI * ((b[:, None] * b[None, :]) % 128) / 128
    cos, sin = np.cos(angle), np.sin(angle)
    return np.block([[cos, -sin], [sin, cos]])


def matrix_inverse():
    return matrix_forward().T


def matrix_first_slot():
    b = np.arange(128)[:, None]
    m = np.arange(64)[None, :]
    low = TWO_PI * ((b * 32 * m) % N) / N
    high = TWO_PI * ((b * (16 + 32 * m)) % N) / N
    out = np.zeros((256, 256))
    out[:128, :64] = np.cos(low)
    out[:128, 128:192] = -np.sin(low)
    out[:128, 128] = 1.0 - 2.0 * (np.arange(128) % 2)
    out[128:, 64:128] = np.cos(high)
    out[128:, 192:] = -np.sin(high)
    return out


def matrix_first_slot_inverse():
    out = 2.0 * matrix_first_slot().T
    out[0] *= 0.5
    out[128] *= 0.5
    return out


def cosine_coefficients():
    nodes = 0.125 * (1.0 - np.cos(np.pi * (np.arange(64) + 0.5) / 64))
    values = np.cos(TWO_PI * np.sqrt(nodes))
    fit = np.polynomial.chebyshev.Chebyshev.fit(nodes, values, 6, domain=[0.0, 0.25])
    return [float(v) for v in fit.convert(kind=np.polynomial.Polynomial).coef]


COSINE = cosine_coefficients()


def turned(re, im, index, length, sign):
    index = index % length
    if index == 0:
        return re, im
    if 4 * index == length:
        if im is None:
            return None, (re if sign > 0 else -re)
        return (-im, re) if sign > 0 else (im, -re)
    c = math.cos(TWO_PI * index / length)
    s = sign * math.sin(TWO_PI * index / length)
    if im is None:
        return re * c, re * s
    if 8 * index == length:
        return ((re - im) * c, (re + im) * c) if sign > 0 else ((re + im) * c, (im - re) * c)
    if 8 * index == 3 * length:
        c = -c
        return (-((re + im) * c), (re - im) * c) if sign > 0 else ((im - re) * c, -((re + im) * c))
    return re * c - im * s, re * s + im * c


def plus(a, b):
    return b if a is None else (a if b is None else a + b)


def minus(a, b):
    if b is None:
        return a
    return -b if a is None else a - b


def real_forward(values):
    length = len(values)
    if length == 2:
        return [(values[0] + values[1], None), (values[0] - values[1], None)]
    even = real_forward(values[0::2])
    odd = real_forward(values[1::2])
    out = [None] * (length // 2 + 1)
    for k in range(length // 4 + 1):
        er, ei = even[k]
        tr, ti = turned(odd[k][0], odd[k][1], k, length, -1)
        out[k] = (plus(er, tr), plus(ei, ti))
        if 4 * k != length:
            out[length // 2 - k] = (minus(er, tr), minus(ti, ei))
    return out


def real_inverse(spectrum):
    length = 2 * (len(spectrum) - 1)
    if length == 2:
        return [spectrum[0][0] + spectrum[1][0], spectrum[0][0] - spectrum[1][0]]
    even, odd = [], []
    for k in range(length // 4 + 1):
        zr, zi = spectrum[k]
        yr, yi = spectrum[length // 2 - k]
        if 4 * k == length:
            even.append((zr + zr, None))
            odd.append((-(zi + zi), None))
            continue
        even.append((zr + yr, minus(zi, yi)))
        odd.append(turned(zr - yr, plus(zi, yi), k, length, 1))
    out = [None] * length
    out[0::2] = real_inverse(even)
    out[1::2] = real_inverse(odd)
    return out


def complex_sum(values, sign):
    length = len(values)
    if length == 1:
        return values
    even = complex_sum(values[0::2], sign)
    odd = complex_sum(values[1::2], sign)
    out = [None] * length
    for k in range(length // 2):
        er, ei = even[k]
        tr, ti = turned(odd[k][0], odd[k][1], k, length, sign)
        out[k] = (er + tr, ei + ti)
        out[k + length // 2] = (er - tr, ei - ti)
    return out


def parts(value):
    high = value.astype(BF16)
    return high, (value - high.astype(F32)).astype(BF16)


def mm(a, b, transposed=False):
    dims = (((1,), (1,)), ((), ())) if transposed else (((1,), (0,)), ((), ()))
    return lax.dot_general(a, b, dims, preferred_element_type=F32)


def lanes_of(shape):
    return lax.broadcasted_iota(jnp.int32, shape, len(shape) - 1)


def places():
    return lax.axis_index("depth"), lax.axis_index("lat")


def mark_tiles(tiles_ref, hits_ref, lat_place):
    for t in range(40):
        hits_ref[t] = 0.0
    for slot in range(16):
        hits_ref[tiles_ref[slot, lat_place // 2]] = 1.0


def rows_kernel(
    depth_ref, tiles_hbm, vol_hbm, holo_hbm, tw_hbm, wt_hbm, out_ref, mask_ref, tiles_ref, src_ref, tw, wt_ref, y_ref, hits_ref, sems
):
    copies = [
        pltpu.make_async_copy(tiles_hbm, tiles_ref, sems.at[0]),
        pltpu.make_async_copy(vol_hbm, src_ref.at[0:ROWS], sems.at[1]),
        pltpu.make_async_copy(tw_hbm, tw, sems.at[2]),
        pltpu.make_async_copy(holo_hbm, src_ref.at[ROWS : 2 * ROWS], sems.at[3]),
        pltpu.make_async_copy(wt_hbm, wt_ref, sems.at[4]),
    ]
    for copy in copies:
        copy.start()
    depth_place, lat_place = places()
    copies[0].wait()
    mark_tiles(tiles_ref, hits_ref, lat_place)
    for a in range(32):
        mask_ref[a : a + 1, :] = jnp.full((1, 128), hits_ref[a], F32)

    def group(masked, g):
        start = g * 16 + (0 if masked else ROWS)
        rows = slice(start, start + 16)
        values = []
        for a in range(32):
            tile = src_ref[rows, a * TILE : (a + 1) * TILE].astype(F32)
            values.append(tile * mask_ref[a : a + 1, :] if masked else tile)
        base = g * 16 + (0 if masked else 1024)
        spec = real_forward(values)
        at = slice(base, base + 16)
        y_ref[at, :128] = spec[0][0]
        y_ref[at, 128:] = spec[16][0]
        for k in range(1, 16):
            at = slice(base + k * ROWS, base + k * ROWS + 16)
            re, im = spec[k]
            c, s = tw[k : k + 1, :], tw[32 + k : 33 + k, :]
            y_ref[at, :128] = re * c + im * s
            y_ref[at, 128:] = im * c - re * s

    copies[1].wait()
    copies[2].wait()
    for g in range(4):
        group(True, g)
    copies[3].wait()
    copies[4].wait()

    def apply(start, size, high, low):
        w_high, w_low = wt_ref[0, pl.ds(start, size), :], wt_ref[1, pl.ds(start, size), :]
        return mm(w_high, high, True) + (mm(w_high, low, True) + mm(w_low, high, True))

    for g in range(4):
        group(False, g)
    for sg in range(4):
        high, low = parts(y_ref[sg * 256 : (sg + 1) * 256, :])
        o = apply(0, 256, high, low)
        for h in range(2):
            part = o[:, h * 128 : (h + 1) * 128]
            if sg == 0 and h == 0:
                first = apply(256, 256, high[:128], low[:128])
                part = jnp.where(lanes_of(part.shape) < ROWS, first, part)
            for c in range(2):
                out_ref[pl.ds(sg * 640 + c * 2 + h, 128, stride=5), :] = part[c * 128 : (c + 1) * 128]

    depth = depth_ref[0]
    half, slot_low = depth_place // 4, depth_place % 4
    for sg in range(4):
        slot = sg * 4 + slot_low
        y = y_ref[pl.ds(pl.multiple_of(1024 + slot * ROWS, ROWS), ROWS), :]
        high, low = parts(jnp.concatenate([y, y], axis=0))
        start = half * 128
        if sg == 0:
            start = start + jnp.where(slot_low == 0, 256, 0)
        o = apply(pl.multiple_of(start, 128), 128, high, low)
        out_ref[pl.ds(sg * 640 + 4, 128, stride=5), :] = jnp.where(lanes_of(o.shape) < ROWS, o, depth)


def signed(index):
    return jnp.where(index < N // 2, index, index - N)


def cosine(turns):
    rest = turns - jnp.round(turns)
    square = rest * rest
    value = COSINE[-1] * square + COSINE[-2]
    for coefficient in COSINE[-3::-1]:
        value = value * square + coefficient
    return value


def columns_kernel(in_ref, tc_ref, ts_ref, w_ref, wi_ref, out_ref, x_ref, zr_ref, zi_ref, bend_ref):
    depth_place, lat_place = places()
    place = lat_place * PLANES + depth_place
    first = place == 0
    slot_group, col = place // 128, place % 128
    left = lanes_of((8, 128)) < ROWS
    fourth = lax.broadcasted_iota(jnp.int32, (8, 128), 0) % 4 == 0
    zero = jnp.zeros((8, 128), F32)

    def swap(value):
        return pltpu.roll(value, ROWS, 1)

    def exchanged(p, q):
        middle = swap(jnp.where(left, q, p))
        return jnp.where(left, p, middle), jnp.where(left, middle, q)

    def x_at(g, a, c):
        return slice(g * 512 + a * 16 + c * 8, g * 512 + a * 16 + c * 8 + 8)

    def received(a, upper, q):
        return in_ref[pl.ds(a * 80 + upper * 40 + q, 8, stride=5), :]

    def store_spectrum(g, k, re, im):
        if k > 0:
            c, s = tc_ref[k : k + 1, :], ts_ref[k : k + 1, :]
            re, im = re * c + im * s, im * c - re * s
        at = pl.ds(g * 320 + k, 8, stride=40)
        zr_ref[at, :] = re
        zi_ref[at, :] = im

    ky = lax.broadcasted_iota(jnp.int32, (32, 128), 0) + 32 * lax.broadcasted_iota(jnp.int32, (32, 128), 1)
    uy = signed(ky).astype(F32) * (WAVE_RATIO / N)
    for g in range(5):
        if g == 4:
            kx = jnp.full((32, 128), -(N // 2), jnp.int32)
        else:
            slot = slot_group * 4 + g
            kx = slot + 32 * col
            if g == 0:
                kx = jnp.where(slot == 0, jnp.where(col < 64, 32 * col, 16 + 32 * (col - 64)), kx)
            kx = signed(jnp.full((32, 128), kx, jnp.int32))
        ux = kx.astype(F32) * (WAVE_RATIO / N)
        squared = uy * uy + ux * ux
        bending = squared / (1.0 + jnp.sqrt(1.0 - squared))
        bend_ref[g * 32 : (g + 1) * 32, :] = 0.5 * (squared + bending * bending)

    def forward(h):
        packed = jnp.logical_and(first, left)
        halves = []
        for upper in range(2):
            values = []
            for a in range(32):
                re, im = received(a, upper, h), received(a, upper, 2 + h)
                values.append((re, jnp.where(packed, zero, im) if h == 0 else im))
            halves.append(complex_sum(values, -1))
        for k in range(32):
            lower, upper = halves[0][k], halves[1][k]
            for number, column in enumerate(zip(*[exchanged(p, q) for p, q in zip(lower, upper)])):
                store_spectrum(2 * h + number, k, *column)


    for a in range(32):
        both = jnp.where(left, received(a, 0, 4), swap(received(a, 1, 4)))
        x_ref[x_at(0, a, 0), :] = both
        x_ref[x_at(0, a, 1), :] = jnp.where(jnp.logical_and(first, fourth), zero, pltpu.roll(both, 4, 0))
        both = jnp.where(left, received(a, 0, 2), swap(received(a, 1, 2)))
        x_ref[x_at(1, a, 0), :] = jnp.where(first, both, zero)
        x_ref[x_at(1, a, 1), :] = zero

    for g in range(2):
        values = [(x_ref[x_at(g, a, 0), :], x_ref[x_at(g, a, 1), :]) for a in range(32)]
        for k, (re, im) in enumerate(complex_sum(values, -1)):
            store_spectrum(4 + g, k, re, im)

    def product(start, size, table):
        slabs = [slice((r // 32) * 40, (r // 32) * 40 + 32) for r in range(start, start + size, 32)]
        pairs = [parts(jnp.concatenate([ref[at, :] for at in slabs], axis=0)) for ref in (zr_ref, zi_ref)]
        high = jnp.concatenate([pairs[0][0], pairs[1][0]], axis=1)
        low = jnp.concatenate([pairs[0][1], pairs[1][1]], axis=1)
        value = mm(high, table[0]) + (mm(low, table[0]) + mm(high, table[1]))
        for i, at in enumerate(slabs):
            zr_ref[at, :] = value[i * 32 : (i + 1) * 32, :128]
            zi_ref[at, :] = value[i * 32 : (i + 1) * 32, 128:]

    forward(0)
    product(1024, 512, w_ref)
    forward(1)
    product(0, 512, w_ref)
    product(512, 512, w_ref)

    scales = []
    for p in range(PLANES):
        row = jnp.broadcast_to(in_ref[p * 5 + 4 : p * 5 + 5, :], (8, 128))
        scales.append(DEPTH_SCALE * jnp.where(left, swap(row), row))
    gain = STEP_SIZE * 2.0 / (N * N)

    def mix(index):
        g = 5 if index == 4 else index
        for j in range(4):
            bend = bend_ref[index * 32 + j * 8 : index * 32 + j * 8 + 8, :]
            waves = [cosine(scale * bend) for scale in scales]
            rows = [slice(g * 320 + p * 40 + j * 8, g * 320 + p * 40 + j * 8 + 8) for p in range(PLANES)]
            at = slice(1280 + index * 40 + j * 8, 1280 + index * 40 + j * 8 + 8)
            scaled = []
            for ref in (zr_ref, zi_ref):
                terms = [wave * ref[row, :] for wave, row in zip(waves, rows)]
                while len(terms) > 1:
                    terms = [p + q for p, q in zip(terms[0::2], terms[1::2])]
                scaled.append((ref[at, :] - 2.0 * terms[0]) * gain)
            if index == 4:
                scaled = [jnp.where(first, value, zero) for value in scaled]
            for p, row in enumerate(rows):
                re, im = waves[p] * scaled[0], waves[p] * scaled[1]
                if index == 0:
                    other = slice(row.start + 1600, row.stop + 1600)
                    re, im = re - zi_ref[other, :], im + zr_ref[other, :]
                zr_ref[row, :] = re
                zi_ref[row, :] = im

    mix(4)
    mix(0)
    product(0, 256, wi_ref)
    mix(1)
    product(256, 256, wi_ref)
    mix(2)
    product(512, 256, wi_ref)
    mix(3)
    product(768, 256, wi_ref)

    for h in range(2):
        lower, upper = [], []
        for k in range(32):
            columns = []
            for g in (2 * h, 2 * h + 1):
                at = pl.ds(g * 320 + k, 8, stride=40)
                re, im = zr_ref[at, :], zi_ref[at, :]
                if k > 0:
                    c, s = tc_ref[k : k + 1, :], ts_ref[k : k + 1, :]
                    re, im = re * c - im * s, im * c + re * s
                columns.append((re, im))
            halves = list(zip(*[exchanged(p, q) for p, q in zip(*columns)]))
            lower.append(halves[0])
            upper.append(halves[1])
        for number, values in enumerate((lower, upper)):
            for a, (re, im) in enumerate(complex_sum(values, 1)):
                out_ref[pl.ds(a * 64 + number * 32 + h, 8, stride=4), :] = re
                out_ref[pl.ds(a * 64 + number * 32 + 2 + h, 8, stride=4), :] = im


def update_kernel(mask_ref, vol_ref, in_ref, tc_ref, ts_ref, wi_ref, out_hbm, y_ref, high_ref, low_ref, new_ref, sems):
    def apply(which, high, low):
        w_high, w_low = wi_ref[0, which], wi_ref[1, which]
        return mm(high, w_high) + (mm(low, w_high) + mm(high, w_low))

    for sg in range(4):
        blocks = [[in_ref[pl.ds(sg * 512 + c * 2 + h, 128, stride=4), :].T for c in range(2)] for h in range(2)]
        high, low = parts(jnp.concatenate([jnp.concatenate(pair, axis=1) for pair in blocks], axis=0))
        high_ref[sg * 256 : (sg + 1) * 256, :] = high
        low_ref[sg * 256 : (sg + 1) * 256, :] = low
    y_ref[0:64, :] = apply(1, high_ref[0:64, :], low_ref[0:64, :])

    def copy_out(g):
        rows = slice(g * 16, g * 16 + 16)
        return pltpu.make_async_copy(new_ref.at[rows], out_hbm.at[rows], sems.at[g])

    for g in range(4):
        rows = slice(g * 16, g * 16 + 16)
        spots = [slice(g * 16 + k * ROWS, g * 16 + k * ROWS + 16) for k in range(1, 16)]
        value = apply(0, *[jnp.concatenate([ref[at, :] for at in spots], axis=0) for ref in (high_ref, low_ref)])
        spec = [(y_ref[rows, :128], None)]
        for k in range(1, 16):
            at = slice((k - 1) * 16, k * 16)
            re, im = value[at, :128], value[at, 128:]
            c, s = tc_ref[k : k + 1, :], ts_ref[k : k + 1, :]
            spec.append((re * c - im * s, im * c + re * s))
        spec.append((y_ref[rows, 128:], None))
        for a, step in enumerate(real_inverse(spec)):
            cols = slice(a * TILE, (a + 1) * TILE)
            support = mask_ref[a : a + 1, :]
            updated = vol_ref[rows, cols].astype(F32) * support + step
            new_ref[rows, cols] = support * (updated - jnp.clip(updated, -THRESHOLD, THRESHOLD))
        copy_out(g).start()
    for g in range(4):
        copy_out(g).wait()


def call(kernel, out_shapes, operands, places, scratch):
    spaces = {"s": pltpu.SMEM, "v": pltpu.VMEM, "h": pltpu.HBM}
    specs = [pl.BlockSpec(memory_space=spaces[place]) for place in places]
    operands = [
        pltpu.with_memory_space_constraint(x, pltpu.HBM) if place == "h" else x for x, place in zip(operands, places)
    ]
    return pl.pallas_call(
        kernel,
        out_shape=[jax.ShapeDtypeStruct(shape, F32) for shape in out_shapes],
        in_specs=specs[: len(operands)],
        out_specs=specs[len(operands) :],
        scratch_shapes=scratch,
        compiler_params=pltpu.CompilerParams(vmem_limit_bytes=VMEM_LIMIT),
    )(*operands)


def rows_step(tiles, depth, volume, hologram):
    wt = np.concatenate([matrix_forward().T, matrix_first_slot().T], axis=0)
    return call(
        rows_kernel,
        [(2560, 128), (32, 128)],
        (depth, tiles, volume, hologram, np.concatenate(twist_tables()), split_np(wt)),
        "shhhhhvv",
        [
            pltpu.SMEM((16, 32), jnp.int32),
            pltpu.VMEM((2 * ROWS, N), BF16),
            pltpu.VMEM((64, 128), F32),
            pltpu.VMEM((2, 512, 256), BF16),
            pltpu.VMEM((2048, 256), F32),
            pltpu.SMEM((40,), F32),
            pltpu.SemaphoreType.DMA((5,)),
        ],
    )


def columns_step(received):
    tc, ts = twist_tables()
    return call(
        columns_kernel,
        [(2048, 128)],
        (received, tc, ts, split_np(matrix_forward()), split_np(matrix_inverse())),
        "vvvvvv",
        [
            pltpu.VMEM((1024, 128), F32),
            pltpu.VMEM((1920, 128), F32),
            pltpu.VMEM((1920, 128), F32),
            pltpu.VMEM((160, 128), F32),
        ],
    )


def update_step(mask, volume, received):
    tc, ts = twist_tables()
    wi = split_np(np.stack([matrix_inverse(), matrix_first_slot_inverse()]))
    return call(
        update_kernel,
        [(ROWS, N)],
        (mask, volume, received, tc, ts, wi),
        "vvvvvvh",
        [pltpu.VMEM((64, 256), F32), pltpu.VMEM((1024, 256), BF16), pltpu.VMEM((1024, 256), BF16), pltpu.VMEM((ROWS, N), F32), pltpu.SemaphoreType.DMA((4,))],
    )


def exchange(value, shape):
    moved = lax.all_to_all(value.reshape(shape), ("lat", "depth"), split_axis=0, concat_axis=0, tiled=True)
    return moved.reshape(value.shape)


def body(volume, hologram, plane_depth, tile_list):
    tiles, volume = tile_list[0].T, volume[0]
    spectra, mask = rows_step(tiles, plane_depth, volume, hologram)
    spectra = exchange(spectra, (512, 1, 640))
    (filtered,) = columns_step(spectra)
    filtered = exchange(filtered, (512, 4, 128))
    (updated,) = update_step(mask, volume, filtered)
    return updated[None]


def solution(mesh):
    return jax.shard_map(
        body,
        mesh=mesh,
        in_specs=(P("depth", "lat", None), P("lat", None), P("depth"), P("depth", None, None)),
        out_specs=P("depth", "lat", None),
        check_vma=False,
    )
```

```python
import math

import jax
import jax.numpy as jnp
import ml_dtypes
import numpy as np
from jax import lax
from jax.experimental import pallas as pl
from jax.experimental.pallas import tpu as pltpu
from jax.sharding import PartitionSpec as P


TILE = 128
N = 4096
ROWS = 64
PLANES = 8
TWO_PI = 2.0 * math.pi
WAVE_RATIO = 0.266
DEPTH_SCALE = 0.001 / 5.32e-07
STEP_SIZE = 0.1
THRESHOLD = 0.25
F32 = jnp.float32
BF16 = jnp.bfloat16
VMEM_LIMIT = 48 * 1024 * 1024


def split_np(table):
    table = np.asarray(table, np.float64)
    high = table.astype(ml_dtypes.bfloat16)
    low = (table - high.astype(np.float64)).astype(ml_dtypes.bfloat16)
    return np.stack([high, low])


def twist_tables():
    k = np.arange(32)[:, None]
    b = np.arange(128)[None, :]
    angle = TWO_PI * ((k * b) % N) / N
    return np.cos(angle).astype(np.float32), np.sin(angle).astype(np.float32)


def matrix_forward():
    b = np.arange(128)
    angle = TWO_PI * ((b[:, None] * b[None, :]) % 128) / 128
    cos, sin = np.cos(angle), np.sin(angle)
    return np.block([[cos, -sin], [sin, cos]])


def matrix_inverse():
    return matrix_forward().T


def matrix_first_slot():
    b = np.arange(128)[:, None]
    m = np.arange(64)[None, :]
    low = TWO_PI * ((b * 32 * m) % N) / N
    high = TWO_PI * ((b * (16 + 32 * m)) % N) / N
    out = np.zeros((256, 256))
    out[:128, :64] = np.cos(low)
    out[:128, 128:192] = -np.sin(low)
    out[:128, 128] = 1.0 - 2.0 * (np.arange(128) % 2)
    out[128:, 64:128] = np.cos(high)
    out[128:, 192:] = -np.sin(high)
    return out


def matrix_first_slot_inverse():
    out = 2.0 * matrix_first_slot().T
    out[0] *= 0.5
    out[128] *= 0.5
    return out


def cosine_coefficients():
    nodes = 0.125 * (1.0 - np.cos(np.pi * (np.arange(64) + 0.5) / 64))
    values = np.cos(TWO_PI * np.sqrt(nodes))
    fit = np.polynomial.chebyshev.Chebyshev.fit(nodes, values, 6, domain=[0.0, 0.25])
    return [float(v) for v in fit.convert(kind=np.polynomial.Polynomial).coef]


COSINE = cosine_coefficients()


def turned(re, im, index, length, sign):
    index = index % length
    if index == 0:
        return re, im
    if 4 * index == length:
        if im is None:
            return None, (re if sign > 0 else -re)
        return (-im, re) if sign > 0 else (im, -re)
    c = math.cos(TWO_PI * index / length)
    s = sign * math.sin(TWO_PI * index / length)
    if im is None:
        return re * c, re * s
    if 8 * index == length:
        return ((re - im) * c, (re + im) * c) if sign > 0 else ((re + im) * c, (im - re) * c)
    if 8 * index == 3 * length:
        c = -c
        return (-((re + im) * c), (re - im) * c) if sign > 0 else ((im - re) * c, -((re + im) * c))
    return re * c - im * s, re * s + im * c


def plus(a, b):
    return b if a is None else (a if b is None else a + b)


def minus(a, b):
    if b is None:
        return a
    return -b if a is None else a - b


def real_forward(values):
    length = len(values)
    if length == 2:
        return [(values[0] + values[1], None), (values[0] - values[1], None)]
    even = real_forward(values[0::2])
    odd = real_forward(values[1::2])
    out = [None] * (length // 2 + 1)
    for k in range(length // 4 + 1):
        er, ei = even[k]
        tr, ti = turned(odd[k][0], odd[k][1], k, length, -1)
        out[k] = (plus(er, tr), plus(ei, ti))
        if 4 * k != length:
            out[length // 2 - k] = (minus(er, tr), minus(ti, ei))
    return out


def real_inverse(spectrum):
    length = 2 * (len(spectrum) - 1)
    if length == 2:
        return [spectrum[0][0] + spectrum[1][0], spectrum[0][0] - spectrum[1][0]]
    even, odd = [], []
    for k in range(length // 4 + 1):
        zr, zi = spectrum[k]
        yr, yi = spectrum[length // 2 - k]
        if 4 * k == length:
            even.append((zr + zr, None))
            odd.append((-(zi + zi), None))
            continue
        even.append((zr + yr, minus(zi, yi)))
        odd.append(turned(zr - yr, plus(zi, yi), k, length, 1))
    out = [None] * length
    out[0::2] = real_inverse(even)
    out[1::2] = real_inverse(odd)
    return out


def complex_sum(values, sign):
    length = len(values)
    if length == 1:
        return values
    even = complex_sum(values[0::2], sign)
    odd = complex_sum(values[1::2], sign)
    out = [None] * length
    for k in range(length // 2):
        er, ei = even[k]
        tr, ti = turned(odd[k][0], odd[k][1], k, length, sign)
        out[k] = (er + tr, ei + ti)
        out[k + length // 2] = (er - tr, ei - ti)
    return out


def parts(value):
    high = value.astype(BF16)
    return high, (value - high.astype(F32)).astype(BF16)


def mm(a, b, transposed=False):
    dims = (((1,), (1,)), ((), ())) if transposed else (((1,), (0,)), ((), ()))
    return lax.dot_general(a, b, dims, preferred_element_type=F32)


def lanes_of(shape):
    return lax.broadcasted_iota(jnp.int32, shape, len(shape) - 1)


def places():
    return lax.axis_index("depth"), lax.axis_index("lat")


def mark_tiles(tiles_ref, hits_ref, lat_place):
    for t in range(40):
        hits_ref[t] = 0.0
    for slot in range(16):
        hits_ref[tiles_ref[slot, lat_place // 2]] = 1.0


def rows_kernel(
    depth_ref, tiles_hbm, vol_hbm, holo_hbm, tw_hbm, wt_hbm, out_ref, mask_ref, tiles_ref, src_ref, tw, wt_ref, y_ref, hits_ref, sems
):
    copies = [
        pltpu.make_async_copy(tiles_hbm, tiles_ref, sems.at[0]),
        pltpu.make_async_copy(vol_hbm, src_ref.at[0:ROWS], sems.at[1]),
        pltpu.make_async_copy(tw_hbm, tw, sems.at[2]),
        pltpu.make_async_copy(holo_hbm, src_ref.at[ROWS : 2 * ROWS], sems.at[3]),
        pltpu.make_async_copy(wt_hbm, wt_ref, sems.at[4]),
    ]
    for copy in copies:
        copy.start()
    depth_place, lat_place = places()
    copies[0].wait()
    mark_tiles(tiles_ref, hits_ref, lat_place)
    for a in range(32):
        mask_ref[a : a + 1, :] = jnp.full((1, 128), hits_ref[a], F32)

    def group(masked, g):
        start = g * 16 + (0 if masked else ROWS)
        rows = slice(start, start + 16)
        values = []
        for a in range(32):
            tile = src_ref[rows, a * TILE : (a + 1) * TILE].astype(F32)
            values.append(tile * mask_ref[a : a + 1, :] if masked else tile)
        base = g * 16 + (0 if masked else 1024)
        spec = real_forward(values)
        at = slice(base, base + 16)
        y_ref[at, :128] = spec[0][0]
        y_ref[at, 128:] = spec[16][0]
        for k in range(1, 16):
            at = slice(base + k * ROWS, base + k * ROWS + 16)
            re, im = spec[k]
            c, s = tw[k : k + 1, :], tw[32 + k : 33 + k, :]
            y_ref[at, :128] = re * c + im * s
            y_ref[at, 128:] = im * c - re * s

    copies[1].wait()
    copies[2].wait()
    for g in range(4):
        group(True, g)
    copies[3].wait()
    copies[4].wait()

    def apply(start, size, high, low):
        w_high, w_low = wt_ref[0, pl.ds(start, size), :], wt_ref[1, pl.ds(start, size), :]
        return mm(w_high, high, True) + (mm(w_high, low, True) + mm(w_low, high, True))

    for g in range(4):
        group(False, g)
    for sg in range(4):
        high, low = parts(y_ref[sg * 256 : (sg + 1) * 256, :])
        o = apply(0, 256, high, low)
        for h in range(2):
            part = o[:, h * 128 : (h + 1) * 128]
            if sg == 0 and h == 0:
                first = apply(256, 256, high[:128], low[:128])
                part = jnp.where(lanes_of(part.shape) < ROWS, first, part)
            for c in range(2):
                out_ref[pl.ds(sg * 640 + c * 2 + h, 128, stride=5), :] = part[c * 128 : (c + 1) * 128]

    depth = depth_ref[0]
    half, slot_low = depth_place // 4, depth_place % 4
    for sg in range(4):
        slot = sg * 4 + slot_low
        y = y_ref[pl.ds(pl.multiple_of(1024 + slot * ROWS, ROWS), ROWS), :]
        high, low = parts(jnp.concatenate([y, y], axis=0))
        start = half * 128
        if sg == 0:
            start = start + jnp.where(slot_low == 0, 256, 0)
        o = apply(pl.multiple_of(start, 128), 128, high, low)
        out_ref[pl.ds(sg * 640 + 4, 128, stride=5), :] = jnp.where(lanes_of(o.shape) < ROWS, o, depth)


def signed(index):
    return jnp.where(index < N // 2, index, index - N)


def cosine(turns):
    rest = turns - jnp.round(turns)
    square = rest * rest
    value = COSINE[-1] * square + COSINE[-2]
    for coefficient in COSINE[-3::-1]:
        value = value * square + coefficient
    return value


def columns_kernel(in_ref, tc_ref, ts_ref, w_ref, wi_ref, out_ref, x_ref, zr_ref, zi_ref, bend_ref):
    depth_place, lat_place = places()
    place = lat_place * PLANES + depth_place
    first = place == 0
    slot_group, col = place // 128, place % 128
    left = lanes_of((8, 128)) < ROWS
    fourth = lax.broadcasted_iota(jnp.int32, (8, 128), 0) % 4 == 0
    zero = jnp.zeros((8, 128), F32)

    def swap(value):
        return pltpu.roll(value, ROWS, 1)

    def exchanged(p, q):
        middle = swap(jnp.where(left, q, p))
        return jnp.where(left, p, middle), jnp.where(left, middle, q)

    def x_at(g, a, c):
        return slice(g * 512 + a * 16 + c * 8, g * 512 + a * 16 + c * 8 + 8)

    def received(a, upper, q):
        return in_ref[pl.ds(a * 80 + upper * 40 + q, 8, stride=5), :]

    def store_spectrum(g, k, re, im):
        if k > 0:
            c, s = tc_ref[k : k + 1, :], ts_ref[k : k + 1, :]
            re, im = re * c + im * s, im * c - re * s
        at = pl.ds(g * 320 + k, 8, stride=40)
        zr_ref[at, :] = re
        zi_ref[at, :] = im

    ky = lax.broadcasted_iota(jnp.int32, (32, 128), 0) + 32 * lax.broadcasted_iota(jnp.int32, (32, 128), 1)
    uy = signed(ky).astype(F32) * (WAVE_RATIO / N)
    for g in range(5):
        if g == 4:
            kx = jnp.full((32, 128), -(N // 2), jnp.int32)
        else:
            slot = slot_group * 4 + g
            kx = slot + 32 * col
            if g == 0:
                kx = jnp.where(slot == 0, jnp.where(col < 64, 32 * col, 16 + 32 * (col - 64)), kx)
            kx = signed(jnp.full((32, 128), kx, jnp.int32))
        ux = kx.astype(F32) * (WAVE_RATIO / N)
        squared = uy * uy + ux * ux
        bending = squared / (1.0 + jnp.sqrt(1.0 - squared))
        bend_ref[g * 32 : (g + 1) * 32, :] = 0.5 * (squared + bending * bending)

    def forward(h):
        packed = jnp.logical_and(first, left)
        halves = []
        for upper in range(2):
            values = []
            for a in range(32):
                re, im = received(a, upper, h), received(a, upper, 2 + h)
                values.append((re, jnp.where(packed, zero, im) if h == 0 else im))
            halves.append(complex_sum(values, -1))
        for k in range(32):
            lower, upper = halves[0][k], halves[1][k]
            for number, column in enumerate(zip(*[exchanged(p, q) for p, q in zip(lower, upper)])):
                store_spectrum(2 * h + number, k, *column)


    for a in range(32):
        both = jnp.where(left, received(a, 0, 4), swap(received(a, 1, 4)))
        x_ref[x_at(0, a, 0), :] = both
        x_ref[x_at(0, a, 1), :] = jnp.where(jnp.logical_and(first, fourth), zero, pltpu.roll(both, 4, 0))
        both = jnp.where(left, received(a, 0, 2), swap(received(a, 1, 2)))
        x_ref[x_at(1, a, 0), :] = jnp.where(first, both, zero)
        x_ref[x_at(1, a, 1), :] = zero

    for g in range(2):
        values = [(x_ref[x_at(g, a, 0), :], x_ref[x_at(g, a, 1), :]) for a in range(32)]
        for k, (re, im) in enumerate(complex_sum(values, -1)):
            store_spectrum(4 + g, k, re, im)

    def product(start, size, table):
        slabs = [slice((r // 32) * 40, (r // 32) * 40 + 32) for r in range(start, start + size, 32)]
        pairs = [parts(jnp.concatenate([ref[at, :] for at in slabs], axis=0)) for ref in (zr_ref, zi_ref)]
        high = jnp.concatenate([pairs[0][0], pairs[1][0]], axis=1)
        low = jnp.concatenate([pairs[0][1], pairs[1][1]], axis=1)
        value = mm(high, table[0]) + (mm(low, table[0]) + mm(high, table[1]))
        for i, at in enumerate(slabs):
            zr_ref[at, :] = value[i * 32 : (i + 1) * 32, :128]
            zi_ref[at, :] = value[i * 32 : (i + 1) * 32, 128:]

    forward(0)
    product(1024, 512, w_ref)
    forward(1)
    product(0, 512, w_ref)

    scales = []
    for p in range(PLANES):
        row = jnp.broadcast_to(in_ref[p * 5 + 4 : p * 5 + 5, :], (8, 128))
        scales.append(DEPTH_SCALE * jnp.where(left, swap(row), row))
    gain = STEP_SIZE * 2.0 / (N * N)

    def backward(h):
        lower, upper = [], []
        for k in range(32):
            columns = []
            for g in (2 * h, 2 * h + 1):
                at = pl.ds(g * 320 + k, 8, stride=40)
                re, im = zr_ref[at, :], zi_ref[at, :]
                if k > 0:
                    c, s = tc_ref[k : k + 1, :], ts_ref[k : k + 1, :]
                    re, im = re * c - im * s, im * c + re * s
                columns.append((re, im))
            halves = list(zip(*[exchanged(p, q) for p, q in zip(*columns)]))
            lower.append(halves[0])
            upper.append(halves[1])
        for number, values in enumerate((lower, upper)):
            for a, (re, im) in enumerate(complex_sum(values, 1)):
                out_ref[pl.ds(a * 64 + number * 32 + h, 8, stride=4), :] = re
                out_ref[pl.ds(a * 64 + number * 32 + 2 + h, 8, stride=4), :] = im

    def mix(index):
        g = 5 if index == 4 else index
        for j in range(4):
            bend = bend_ref[index * 32 + j * 8 : index * 32 + j * 8 + 8, :]
            waves = [cosine(scale * bend) for scale in scales]
            rows = [slice(g * 320 + p * 40 + j * 8, g * 320 + p * 40 + j * 8 + 8) for p in range(PLANES)]
            at = slice(1280 + index * 40 + j * 8, 1280 + index * 40 + j * 8 + 8)
            scaled = []
            for ref in (zr_ref, zi_ref):
                terms = [wave * ref[row, :] for wave, row in zip(waves, rows)]
                while len(terms) > 1:
                    terms = [p + q for p, q in zip(terms[0::2], terms[1::2])]
                scaled.append((ref[at, :] - 2.0 * terms[0]) * gain)
            if index == 4:
                scaled = [jnp.where(first, value, zero) for value in scaled]
            for p, row in enumerate(rows):
                re, im = waves[p] * scaled[0], waves[p] * scaled[1]
                if index == 0:
                    other = slice(row.start + 1600, row.stop + 1600)
                    re, im = re - zi_ref[other, :], im + zr_ref[other, :]
                zr_ref[row, :] = re
                zi_ref[row, :] = im

    mix(4)
    product(512, 512, w_ref)
    mix(0)
    product(0, 256, wi_ref)
    mix(1)
    product(256, 256, wi_ref)
    mix(2)
    product(512, 256, wi_ref)
    backward(0)
    mix(3)
    product(768, 256, wi_ref)
    backward(1)


def update_kernel(mask_ref, vol_ref, in_ref, tc_ref, ts_ref, wi_ref, out_hbm, y_ref, high_ref, low_ref, new_ref, sems):
    def apply(which, high, low):
        w_high, w_low = wi_ref[0, which], wi_ref[1, which]
        return mm(high, w_high) + (mm(low, w_high) + mm(high, w_low))

    for sg in range(4):
        blocks = [[in_ref[pl.ds(sg * 512 + c * 2 + h, 128, stride=4), :].T for c in range(2)] for h in range(2)]
        high, low = parts(jnp.concatenate([jnp.concatenate(pair, axis=1) for pair in blocks], axis=0))
        high_ref[sg * 256 : (sg + 1) * 256, :] = high
        low_ref[sg * 256 : (sg + 1) * 256, :] = low
    y_ref[0:64, :] = apply(1, high_ref[0:64, :], low_ref[0:64, :])

    def copy_out(g):
        rows = slice(g * 16, g * 16 + 16)
        return pltpu.make_async_copy(new_ref.at[rows], out_hbm.at[rows], sems.at[g])

    for g in range(4):
        rows = slice(g * 16, g * 16 + 16)
        spots = [slice(g * 16 + k * ROWS, g * 16 + k * ROWS + 16) for k in range(1, 16)]
        value = apply(0, *[jnp.concatenate([ref[at, :] for at in spots], axis=0) for ref in (high_ref, low_ref)])
        spec = [(y_ref[rows, :128], None)]
        for k in range(1, 16):
            at = slice((k - 1) * 16, k * 16)
            re, im = value[at, :128], value[at, 128:]
            c, s = tc_ref[k : k + 1, :], ts_ref[k : k + 1, :]
            spec.append((re * c - im * s, im * c + re * s))
        spec.append((y_ref[rows, 128:], None))
        for a, step in enumerate(real_inverse(spec)):
            cols = slice(a * TILE, (a + 1) * TILE)
            support = mask_ref[a : a + 1, :]
            updated = vol_ref[rows, cols].astype(F32) * support + step
            new_ref[rows, cols] = support * (updated - jnp.clip(updated, -THRESHOLD, THRESHOLD))
        copy_out(g).start()
    for g in range(4):
        copy_out(g).wait()


def call(kernel, out_shapes, operands, places, scratch):
    spaces = {"s": pltpu.SMEM, "v": pltpu.VMEM, "h": pltpu.HBM}
    specs = [pl.BlockSpec(memory_space=spaces[place]) for place in places]
    operands = [
        pltpu.with_memory_space_constraint(x, pltpu.HBM) if place == "h" else x for x, place in zip(operands, places)
    ]
    return pl.pallas_call(
        kernel,
        out_shape=[jax.ShapeDtypeStruct(shape, F32) for shape in out_shapes],
        in_specs=specs[: len(operands)],
        out_specs=specs[len(operands) :],
        scratch_shapes=scratch,
        compiler_params=pltpu.CompilerParams(vmem_limit_bytes=VMEM_LIMIT),
    )(*operands)


def rows_step(tiles, depth, volume, hologram):
    wt = np.concatenate([matrix_forward().T, matrix_first_slot().T], axis=0)
    return call(
        rows_kernel,
        [(2560, 128), (32, 128)],
        (depth, tiles, volume, hologram, np.concatenate(twist_tables()), split_np(wt)),
        "shhhhhvv",
        [
            pltpu.SMEM((16, 32), jnp.int32),
            pltpu.VMEM((2 * ROWS, N), BF16),
            pltpu.VMEM((64, 128), F32),
            pltpu.VMEM((2, 512, 256), BF16),
            pltpu.VMEM((2048, 256), F32),
            pltpu.SMEM((40,), F32),
            pltpu.SemaphoreType.DMA((5,)),
        ],
    )


def columns_step(received):
    tc, ts = twist_tables()
    return call(
        columns_kernel,
        [(2048, 128)],
        (received, tc, ts, split_np(matrix_forward()), split_np(matrix_inverse())),
        "vvvvvv",
        [
            pltpu.VMEM((1024, 128), F32),
            pltpu.VMEM((1920, 128), F32),
            pltpu.VMEM((1920, 128), F32),
            pltpu.VMEM((160, 128), F32),
        ],
    )


def update_step(mask, volume, received):
    tc, ts = twist_tables()
    wi = split_np(np.stack([matrix_inverse(), matrix_first_slot_inverse()]))
    return call(
        update_kernel,
        [(ROWS, N)],
        (mask, volume, received, tc, ts, wi),
        "vvvvvvh",
        [pltpu.VMEM((64, 256), F32), pltpu.VMEM((1024, 256), BF16), pltpu.VMEM((1024, 256), BF16), pltpu.VMEM((ROWS, N), F32), pltpu.SemaphoreType.DMA((4,))],
    )


def exchange(value, shape):
    moved = lax.all_to_all(value.reshape(shape), ("lat", "depth"), split_axis=0, concat_axis=0, tiled=True)
    return moved.reshape(value.shape)


def body(volume, hologram, plane_depth, tile_list):
    tiles, volume = tile_list[0].T, volume[0]
    spectra, mask = rows_step(tiles, plane_depth, volume, hologram)
    spectra = exchange(spectra, (512, 1, 640))
    (filtered,) = columns_step(spectra)
    filtered = exchange(filtered, (512, 4, 128))
    (updated,) = update_step(mask, volume, filtered)
    return updated[None]


def solution(mesh):
    return jax.shard_map(
        body,
        mesh=mesh,
        in_specs=(P("depth", "lat", None), P("lat", None), P("depth"), P("depth", None, None)),
        out_specs=P("depth", "lat", None),
        check_vma=False,
    )
```

```python
import math

import jax
import jax.numpy as jnp
import ml_dtypes
import numpy as np
from jax import lax
from jax.experimental import pallas as pl
from jax.experimental.pallas import tpu as pltpu
from jax.sharding import PartitionSpec as P


TILE = 128
N = 4096
ROWS = 64
PLANES = 8
TWO_PI = 2.0 * math.pi
WAVE_RATIO = 0.266
DEPTH_SCALE = 0.001 / 5.32e-07
STEP_SIZE = 0.1
THRESHOLD = 0.25
F32 = jnp.float32
BF16 = jnp.bfloat16
VMEM_LIMIT = 48 * 1024 * 1024


def split_np(table):
    table = np.asarray(table, np.float64)
    high = table.astype(ml_dtypes.bfloat16)
    low = (table - high.astype(np.float64)).astype(ml_dtypes.bfloat16)
    return np.stack([high, low])


def twist_tables():
    k = np.arange(32)[:, None]
    b = np.arange(128)[None, :]
    angle = TWO_PI * ((k * b) % N) / N
    return np.cos(angle).astype(np.float32), np.sin(angle).astype(np.float32)


def matrix_forward():
    b = np.arange(128)
    angle = TWO_PI * ((b[:, None] * b[None, :]) % 128) / 128
    cos, sin = np.cos(angle), np.sin(angle)
    return np.block([[cos, -sin], [sin, cos]])


def matrix_inverse():
    return matrix_forward().T


def matrix_first_slot():
    b = np.arange(128)[:, None]
    m = np.arange(64)[None, :]
    low = TWO_PI * ((b * 32 * m) % N) / N
    high = TWO_PI * ((b * (16 + 32 * m)) % N) / N
    out = np.zeros((256, 256))
    out[:128, :64] = np.cos(low)
    out[:128, 128:192] = -np.sin(low)
    out[:128, 128] = 1.0 - 2.0 * (np.arange(128) % 2)
    out[128:, 64:128] = np.cos(high)
    out[128:, 192:] = -np.sin(high)
    return out


def matrix_first_slot_inverse():
    out = 2.0 * matrix_first_slot().T
    out[0] *= 0.5
    out[128] *= 0.5
    return out


def cosine_coefficients():
    nodes = 0.125 * (1.0 - np.cos(np.pi * (np.arange(64) + 0.5) / 64))
    values = np.cos(TWO_PI * np.sqrt(nodes))
    fit = np.polynomial.chebyshev.Chebyshev.fit(nodes, values, 6, domain=[0.0, 0.25])
    return [float(v) for v in fit.convert(kind=np.polynomial.Polynomial).coef]


COSINE = cosine_coefficients()


def turned(re, im, index, length, sign):
    index = index % length
    if index == 0:
        return re, im
    if 4 * index == length:
        if im is None:
            return None, (re if sign > 0 else -re)
        return (-im, re) if sign > 0 else (im, -re)
    c = math.cos(TWO_PI * index / length)
    s = sign * math.sin(TWO_PI * index / length)
    if im is None:
        return re * c, re * s
    if 8 * index == length:
        return ((re - im) * c, (re + im) * c) if sign > 0 else ((re + im) * c, (im - re) * c)
    if 8 * index == 3 * length:
        c = -c
        return (-((re + im) * c), (re - im) * c) if sign > 0 else ((im - re) * c, -((re + im) * c))
    return re * c - im * s, re * s + im * c


def plus(a, b):
    return b if a is None else (a if b is None else a + b)


def minus(a, b):
    if b is None:
        return a
    return -b if a is None else a - b


def real_forward(values):
    length = len(values)
    if length == 2:
        return [(values[0] + values[1], None), (values[0] - values[1], None)]
    even = real_forward(values[0::2])
    odd = real_forward(values[1::2])
    out = [None] * (length // 2 + 1)
    for k in range(length // 4 + 1):
        er, ei = even[k]
        tr, ti = turned(odd[k][0], odd[k][1], k, length, -1)
        out[k] = (plus(er, tr), plus(ei, ti))
        if 4 * k != length:
            out[length // 2 - k] = (minus(er, tr), minus(ti, ei))
    return out


def real_inverse(spectrum):
    length = 2 * (len(spectrum) - 1)
    if length == 2:
        return [spectrum[0][0] + spectrum[1][0], spectrum[0][0] - spectrum[1][0]]
    even, odd = [], []
    for k in range(length // 4 + 1):
        zr, zi = spectrum[k]
        yr, yi = spectrum[length // 2 - k]
        if 4 * k == length:
            even.append((zr + zr, None))
            odd.append((-(zi + zi), None))
            continue
        even.append((zr + yr, minus(zi, yi)))
        odd.append(turned(zr - yr, plus(zi, yi), k, length, 1))
    out = [None] * length
    out[0::2] = real_inverse(even)
    out[1::2] = real_inverse(odd)
    return out


def complex_sum(values, sign):
    length = len(values)
    if length == 1:
        return values
    even = complex_sum(values[0::2], sign)
    odd = complex_sum(values[1::2], sign)
    out = [None] * length
    for k in range(length // 2):
        er, ei = even[k]
        tr, ti = turned(odd[k][0], odd[k][1], k, length, sign)
        out[k] = (er + tr, ei + ti)
        out[k + length // 2] = (er - tr, ei - ti)
    return out


def parts(value):
    high = value.astype(BF16)
    return high, (value - high.astype(F32)).astype(BF16)


def mm(a, b, transposed=False):
    dims = (((1,), (1,)), ((), ())) if transposed else (((1,), (0,)), ((), ()))
    return lax.dot_general(a, b, dims, preferred_element_type=F32)


def lanes_of(shape):
    return lax.broadcasted_iota(jnp.int32, shape, len(shape) - 1)


def places():
    return lax.axis_index("depth"), lax.axis_index("lat")


def mark_tiles(tiles_ref, hits_ref, lat_place):
    for t in range(40):
        hits_ref[t] = 0.0
    for slot in range(16):
        hits_ref[tiles_ref[slot, lat_place // 2]] = 1.0


def rows_kernel(
    depth_ref, tiles_hbm, vol_hbm, holo_hbm, tw_hbm, wt_hbm, out_ref, mask_ref, tiles_ref, src_ref, tw, wt_ref, y_ref, hits_ref, sems
):
    copies = [
        pltpu.make_async_copy(tiles_hbm, tiles_ref, sems.at[0]),
        pltpu.make_async_copy(vol_hbm, src_ref.at[0:ROWS], sems.at[1]),
        pltpu.make_async_copy(tw_hbm, tw, sems.at[2]),
        pltpu.make_async_copy(holo_hbm, src_ref.at[ROWS : 2 * ROWS], sems.at[3]),
        pltpu.make_async_copy(wt_hbm, wt_ref, sems.at[4]),
    ]
    for copy in copies:
        copy.start()
    depth_place, lat_place = places()
    copies[0].wait()
    mark_tiles(tiles_ref, hits_ref, lat_place)
    for a in range(32):
        mask_ref[a : a + 1, :] = jnp.full((1, 128), hits_ref[a], F32)

    def group(masked, g):
        start = g * 16 + (0 if masked else ROWS)
        rows = slice(start, start + 16)
        values = []
        for a in range(32):
            tile = src_ref[rows, a * TILE : (a + 1) * TILE].astype(F32)
            values.append(tile * mask_ref[a : a + 1, :] if masked else tile)
        base = g * 16 + (0 if masked else 1024)
        spec = real_forward(values)
        at = slice(base, base + 16)
        y_ref[at, :128] = spec[0][0]
        y_ref[at, 128:] = spec[16][0]
        for k in range(1, 16):
            at = slice(base + k * ROWS, base + k * ROWS + 16)
            re, im = spec[k]
            c, s = tw[k : k + 1, :], tw[32 + k : 33 + k, :]
            y_ref[at, :128] = re * c + im * s
            y_ref[at, 128:] = im * c - re * s

    copies[1].wait()
    copies[2].wait()
    for g in range(4):
        group(True, g)
    copies[3].wait()
    copies[4].wait()

    def apply(start, size, high, low):
        w_high, w_low = wt_ref[0, pl.ds(start, size), :], wt_ref[1, pl.ds(start, size), :]
        return mm(w_high, high, True) + (mm(w_high, low, True) + mm(w_low, high, True))

    for g in range(4):
        group(False, g)
    for sg in range(4):
        high, low = parts(y_ref[sg * 256 : (sg + 1) * 256, :])
        o = apply(0, 256, high, low)
        for h in range(2):
            part = o[:, h * 128 : (h + 1) * 128]
            if sg == 0 and h == 0:
                first = apply(256, 256, high[:128], low[:128])
                part = jnp.where(lanes_of(part.shape) < ROWS, first, part)
            for c in range(2):
                out_ref[pl.ds(sg * 640 + c * 2 + h, 128, stride=5), :] = part[c * 128 : (c + 1) * 128]

    depth = depth_ref[0]
    half, slot_low = depth_place // 4, depth_place % 4
    for sg in range(4):
        slot = sg * 4 + slot_low
        y = y_ref[pl.ds(pl.multiple_of(1024 + slot * ROWS, ROWS), ROWS), :]
        high, low = parts(jnp.concatenate([y, y], axis=0))
        start = half * 128
        if sg == 0:
            start = start + jnp.where(slot_low == 0, 256, 0)
        o = apply(pl.multiple_of(start, 128), 128, high, low)
        out_ref[pl.ds(sg * 640 + 4, 128, stride=5), :] = jnp.where(lanes_of(o.shape) < ROWS, o, depth)


def signed(index):
    return jnp.where(index < N // 2, index, index - N)


def cosine(turns):
    rest = turns - jnp.round(turns)
    square = rest * rest
    value = COSINE[-1] * square + COSINE[-2]
    for coefficient in COSINE[-3::-1]:
        value = value * square + coefficient
    return value


def columns_kernel(in_ref, tc_ref, ts_ref, w_ref, wi_ref, out_ref, zr_ref, zi_ref, bend_ref):
    depth_place, lat_place = places()
    place = lat_place * PLANES + depth_place
    first = place == 0
    slot_group, col = place // 128, place % 128
    left = lanes_of((8, 128)) < ROWS
    fourth = lax.broadcasted_iota(jnp.int32, (8, 128), 0) % 4 == 0
    zero = jnp.zeros((8, 128), F32)

    def swap(value):
        return pltpu.roll(value, ROWS, 1)

    def exchanged(p, q):
        middle = swap(jnp.where(left, q, p))
        return jnp.where(left, p, middle), jnp.where(left, middle, q)

    def received(a, upper, q):
        return in_ref[pl.ds(a * 80 + upper * 40 + q, 8, stride=5), :]

    def store_spectrum(g, k, re, im):
        if k > 0:
            c, s = tc_ref[k : k + 1, :], ts_ref[k : k + 1, :]
            re, im = re * c + im * s, im * c - re * s
        at = pl.ds(g * 320 + k, 8, stride=40)
        zr_ref[at, :] = re
        zi_ref[at, :] = im

    ky = lax.broadcasted_iota(jnp.int32, (32, 128), 0) + 32 * lax.broadcasted_iota(jnp.int32, (32, 128), 1)
    uy = signed(ky).astype(F32) * (WAVE_RATIO / N)
    for g in range(5):
        if g == 4:
            kx = jnp.full((32, 128), -(N // 2), jnp.int32)
        else:
            slot = slot_group * 4 + g
            kx = slot + 32 * col
            if g == 0:
                kx = jnp.where(slot == 0, jnp.where(col < 64, 32 * col, 16 + 32 * (col - 64)), kx)
            kx = signed(jnp.full((32, 128), kx, jnp.int32))
        ux = kx.astype(F32) * (WAVE_RATIO / N)
        squared = uy * uy + ux * ux
        bending = squared / (1.0 + jnp.sqrt(1.0 - squared))
        bend_ref[g * 32 : (g + 1) * 32, :] = 0.5 * (squared + bending * bending)

    def forward(h):
        packed = jnp.logical_and(first, left)
        halves = []
        for upper in range(2):
            values = []
            for a in range(32):
                re, im = received(a, upper, h), received(a, upper, 2 + h)
                values.append((re, jnp.where(packed, zero, im) if h == 0 else im))
            halves.append(complex_sum(values, -1))
        for k in range(32):
            lower, upper = halves[0][k], halves[1][k]
            for number, column in enumerate(zip(*[exchanged(p, q) for p, q in zip(lower, upper)])):
                store_spectrum(2 * h + number, k, *column)


    values = []
    for a in range(32):
        both = jnp.where(left, received(a, 0, 4), swap(received(a, 1, 4)))
        values.append((both, jnp.where(jnp.logical_and(first, fourth), zero, pltpu.roll(both, 4, 0))))
    for k, (re, im) in enumerate(complex_sum(values, -1)):
        store_spectrum(4, k, re, im)
    values = []
    for a in range(32):
        both = jnp.where(left, received(a, 0, 2), swap(received(a, 1, 2)))
        values.append(jnp.where(first, both, zero))
    half = real_forward(values)
    for k in range(32):
        re, im = half[min(k, 32 - k)]
        im = zero if im is None else im
        store_spectrum(5, k, re, im if k <= 16 else -im)

    def product(start, size, table):
        slabs = [slice((r // 32) * 40, (r // 32) * 40 + 32) for r in range(start, start + size, 32)]
        pairs = [parts(jnp.concatenate([ref[at, :] for at in slabs], axis=0)) for ref in (zr_ref, zi_ref)]
        high = jnp.concatenate([pairs[0][0], pairs[1][0]], axis=1)
        low = jnp.concatenate([pairs[0][1], pairs[1][1]], axis=1)
        value = mm(high, table[0]) + (mm(low, table[0]) + mm(high, table[1]))
        for i, at in enumerate(slabs):
            zr_ref[at, :] = value[i * 32 : (i + 1) * 32, :128]
            zi_ref[at, :] = value[i * 32 : (i + 1) * 32, 128:]

    forward(0)
    product(1024, 512, w_ref)
    forward(1)
    product(0, 512, w_ref)
    product(512, 512, w_ref)

    scales = []
    for p in range(PLANES):
        row = jnp.broadcast_to(in_ref[p * 5 + 4 : p * 5 + 5, :], (8, 128))
        scales.append(DEPTH_SCALE * jnp.where(left, swap(row), row))
    gain = STEP_SIZE * 2.0 / (N * N)

    def mix(index):
        g = 5 if index == 4 else index
        for j in range(4):
            bend = bend_ref[index * 32 + j * 8 : index * 32 + j * 8 + 8, :]
            waves = [cosine(scale * bend) for scale in scales]
            rows = [slice(g * 320 + p * 40 + j * 8, g * 320 + p * 40 + j * 8 + 8) for p in range(PLANES)]
            at = slice(1280 + index * 40 + j * 8, 1280 + index * 40 + j * 8 + 8)
            scaled = []
            for ref in (zr_ref, zi_ref):
                terms = [wave * ref[row, :] for wave, row in zip(waves, rows)]
                while len(terms) > 1:
                    terms = [p + q for p, q in zip(terms[0::2], terms[1::2])]
                scaled.append((ref[at, :] - 2.0 * terms[0]) * gain)
            if index == 4:
                scaled = [jnp.where(first, value, zero) for value in scaled]
            for p, row in enumerate(rows):
                re, im = waves[p] * scaled[0], waves[p] * scaled[1]
                if index == 0:
                    other = slice(row.start + 1600, row.stop + 1600)
                    re, im = re - zi_ref[other, :], im + zr_ref[other, :]
                zr_ref[row, :] = re
                zi_ref[row, :] = im

    mix(4)
    mix(0)
    product(0, 256, wi_ref)
    mix(1)
    product(256, 256, wi_ref)
    mix(2)
    product(512, 256, wi_ref)
    mix(3)
    product(768, 256, wi_ref)

    for h in range(2):
        lower, upper = [], []
        for k in range(32):
            columns = []
            for g in (2 * h, 2 * h + 1):
                at = pl.ds(g * 320 + k, 8, stride=40)
                re, im = zr_ref[at, :], zi_ref[at, :]
                if k > 0:
                    c, s = tc_ref[k : k + 1, :], ts_ref[k : k + 1, :]
                    re, im = re * c - im * s, im * c + re * s
                columns.append((re, im))
            halves = list(zip(*[exchanged(p, q) for p, q in zip(*columns)]))
            lower.append(halves[0])
            upper.append(halves[1])
        for number, values in enumerate((lower, upper)):
            for a, (re, im) in enumerate(complex_sum(values, 1)):
                out_ref[pl.ds(a * 64 + number * 32 + h, 8, stride=4), :] = re
                out_ref[pl.ds(a * 64 + number * 32 + 2 + h, 8, stride=4), :] = im


def update_kernel(mask_ref, vol_ref, in_ref, tc_ref, ts_ref, wi_ref, out_hbm, y_ref, high_ref, low_ref, new_ref, sems):
    def apply(which, high, low):
        w_high, w_low = wi_ref[0, which], wi_ref[1, which]
        return mm(high, w_high) + (mm(low, w_high) + mm(high, w_low))

    for sg in range(4):
        blocks = [[in_ref[pl.ds(sg * 512 + c * 2 + h, 128, stride=4), :].T for c in range(2)] for h in range(2)]
        high, low = parts(jnp.concatenate([jnp.concatenate(pair, axis=1) for pair in blocks], axis=0))
        high_ref[sg * 256 : (sg + 1) * 256, :] = high
        low_ref[sg * 256 : (sg + 1) * 256, :] = low
    y_ref[0:64, :] = apply(1, high_ref[0:64, :], low_ref[0:64, :])

    def copy_out(g):
        rows = slice(g * 16, g * 16 + 16)
        return pltpu.make_async_copy(new_ref.at[rows], out_hbm.at[rows], sems.at[g])

    for g in range(4):
        rows = slice(g * 16, g * 16 + 16)
        spots = [slice(g * 16 + k * ROWS, g * 16 + k * ROWS + 16) for k in range(1, 16)]
        value = apply(0, *[jnp.concatenate([ref[at, :] for at in spots], axis=0) for ref in (high_ref, low_ref)])
        spec = [(y_ref[rows, :128], None)]
        for k in range(1, 16):
            at = slice((k - 1) * 16, k * 16)
            re, im = value[at, :128], value[at, 128:]
            c, s = tc_ref[k : k + 1, :], ts_ref[k : k + 1, :]
            spec.append((re * c - im * s, im * c + re * s))
        spec.append((y_ref[rows, 128:], None))
        for a, step in enumerate(real_inverse(spec)):
            cols = slice(a * TILE, (a + 1) * TILE)
            support = mask_ref[a : a + 1, :]
            updated = vol_ref[rows, cols].astype(F32) * support + step
            new_ref[rows, cols] = support * (updated - jnp.clip(updated, -THRESHOLD, THRESHOLD))
        copy_out(g).start()
    for g in range(4):
        copy_out(g).wait()


def call(kernel, out_shapes, operands, places, scratch):
    spaces = {"s": pltpu.SMEM, "v": pltpu.VMEM, "h": pltpu.HBM}
    specs = [pl.BlockSpec(memory_space=spaces[place]) for place in places]
    operands = [
        pltpu.with_memory_space_constraint(x, pltpu.HBM) if place == "h" else x for x, place in zip(operands, places)
    ]
    return pl.pallas_call(
        kernel,
        out_shape=[jax.ShapeDtypeStruct(shape, F32) for shape in out_shapes],
        in_specs=specs[: len(operands)],
        out_specs=specs[len(operands) :],
        scratch_shapes=scratch,
        compiler_params=pltpu.CompilerParams(vmem_limit_bytes=VMEM_LIMIT),
    )(*operands)


def rows_step(tiles, depth, volume, hologram):
    wt = np.concatenate([matrix_forward().T, matrix_first_slot().T], axis=0)
    return call(
        rows_kernel,
        [(2560, 128), (32, 128)],
        (depth, tiles, volume, hologram, np.concatenate(twist_tables()), split_np(wt)),
        "shhhhhvv",
        [
            pltpu.SMEM((16, 32), jnp.int32),
            pltpu.VMEM((2 * ROWS, N), BF16),
            pltpu.VMEM((64, 128), F32),
            pltpu.VMEM((2, 512, 256), BF16),
            pltpu.VMEM((2048, 256), F32),
            pltpu.SMEM((40,), F32),
            pltpu.SemaphoreType.DMA((5,)),
        ],
    )


def columns_step(received):
    tc, ts = twist_tables()
    return call(
        columns_kernel,
        [(2048, 128)],
        (received, tc, ts, split_np(matrix_forward()), split_np(matrix_inverse())),
        "vvvvvv",
        [
            pltpu.VMEM((1920, 128), F32),
            pltpu.VMEM((1920, 128), F32),
            pltpu.VMEM((160, 128), F32),
        ],
    )


def update_step(mask, volume, received):
    tc, ts = twist_tables()
    wi = split_np(np.stack([matrix_inverse(), matrix_first_slot_inverse()]))
    return call(
        update_kernel,
        [(ROWS, N)],
        (mask, volume, received, tc, ts, wi),
        "vvvvvvh",
        [pltpu.VMEM((64, 256), F32), pltpu.VMEM((1024, 256), BF16), pltpu.VMEM((1024, 256), BF16), pltpu.VMEM((ROWS, N), F32), pltpu.SemaphoreType.DMA((4,))],
    )


def exchange(value, shape):
    moved = lax.all_to_all(value.reshape(shape), ("lat", "depth"), split_axis=0, concat_axis=0, tiled=True)
    return moved.reshape(value.shape)


def body(volume, hologram, plane_depth, tile_list):
    tiles, volume = tile_list[0].T, volume[0]
    spectra, mask = rows_step(tiles, plane_depth, volume, hologram)
    spectra = exchange(spectra, (512, 1, 640))
    (filtered,) = columns_step(spectra)
    filtered = exchange(filtered, (512, 4, 128))
    (updated,) = update_step(mask, volume, filtered)
    return updated[None]


def solution(mesh):
    return jax.shard_map(
        body,
        mesh=mesh,
        in_specs=(P("depth", "lat", None), P("lat", None), P("depth"), P("depth", None, None)),
        out_specs=P("depth", "lat", None),
        check_vma=False,
    )
```
